32 devices in a mesh: groups: 2 (over y), row: 8 (over z, x), col: 2 (over core).
Axes of the slice: x: 2, y: 2, z: 4, core: 2. Of those that a mesh axis runs over, the one named last changes fastest.
Arguments:
- pair: bfloat16 [48, 24, 128], P(('groups', 'row'), 'col'), parts along dimension 0, may hold values from -6 to 6
- pad_mask: int32 [48], P('groups'), parts along dimension 0, may hold values 0 or 1
- token_count: int32 [2], P('groups'), parts along dimension 0, may hold values from 12 to 24
- norm_gain: float32 [2, 2, 128], replicated, may hold values from 0.1 to 1.9
- proj_in: bfloat16 [2, 128, 512], replicated, may hold values from -0.5 to 0.5
- proj_out: bfloat16 [2, 128, 128], replicated, may hold values from -0.5 to 0.5
- gate_out: bfloat16 [2, 128, 128], replicated, may hold values from -0.5 to 0.5
Outputs:
- pair_out: bfloat16 [48, 24, 128], P(('groups', 'row'), 'col'), parts along dimension 0
The draws below stay inside these ranges and needn't reach their ends.
There are 2 independent parts, one for each index of `groups`. The reference program is written for one: setup_inputs(seed, part) draws one part's arguments, and reference() takes and returns one part's arrays. A program takes and returns all parts, laid end to end along the dimension named above; an argument that names none is the same for every part. Nothing has to cross between parts.
Inputs may be any that keep to these rules, and one draw needn't show every extreme that they name: `token_count`: tokens from this index on are padding.
All inputs are finite; a program needn't handle non-finite values.
Results may differ from the reference program's by a relative error of at most 0.0085.
Values may be sent and summed in bfloat16 or wider, within the bound.
A program may use at most 64 MiB of HBM per device.

```python
import jax
import jax.numpy as jnp
from jax import lax

C = 128
ROWS_DEV = 3
N = 24


def set_ends(drawn, stream_key, least, top_value):
    dims = drawn.shape
    spot = [jax.random.randint(jax.random.fold_in(stream_key, axis), (), 0, dims[axis]) for axis in range(len(dims))]
    drawn = drawn.at[tuple(spot)].set(least)
    longest = dims.index(max(dims))
    spot[longest] = (spot[longest] + 1) % dims[longest]
    return drawn.at[tuple(spot)].set(top_value)


def block_scale(stream_key, extent, pieces, low, top_value):
    factor_of = 1.0
    for axis_at, parts in pieces:
        draws = jax.random.uniform(jax.random.fold_in(jax.random.fold_in(stream_key, 6), axis_at), (parts,), jnp.float32, low / len(pieces), top_value / len(pieces))
        factor_of = factor_of * jnp.repeat(jnp.exp(draws), extent[axis_at] // parts).reshape((-1,) + (1,) * (len(extent) - 1 - axis_at))
    return factor_of


def gaussian(key, extent, scale, limit, shards=(), kind=jnp.bfloat16):
    loudness = block_scale(key, extent, shards, -0.22, 0.18) if shards else 1.0
    values = jax.random.normal(key, extent, jnp.float32) * scale * loudness
    return jnp.minimum(jnp.maximum(values, -limit), limit).astype(kind)


def setup_inputs(seed: int = 0, part: int = 0) -> dict:
    key_list = jax.random.split(jax.random.key(seed), 8)
    own_keys = jax.random.split(jax.random.fold_in(key_list[7], part), 8)
    return {
        "pair": gaussian(own_keys[0], (N, N, C), 1.0, 6.0, ((0, 8), (1, 2))),
        "pad_mask": set_ends((jax.random.randint(own_keys[1], (N,), 0, 8) < 7).astype(jnp.int32), jax.random.fold_in(own_keys[1], 1), 0, 1),
        "token_count": jax.random.randint(own_keys[2], (1,), N // 2, N + 1).astype(jnp.int32),
        "norm_gain": jnp.clip(1.0 + 0.18 * jax.random.normal(key_list[3], (2, 2, C), jnp.float32), 0.1, 1.9),
        "proj_in": gaussian(key_list[4], (2, C, 4 * C), C ** -0.5, 0.5),
        "proj_out": gaussian(key_list[5], (2, C, C), C ** -0.5, 0.5),
        "gate_out": gaussian(key_list[6], (2, C, C), C ** -0.5, 0.5),
    }


EPSILON = 1e-05

def layer_norm(values, gain):
    mean = lax.optimization_barrier(jnp.mean(values, axis=-1, keepdims=True))
    centred = values - mean
    spread = lax.optimization_barrier(jnp.mean(centred * centred, axis=-1, keepdims=True))
    return centred * lax.rsqrt(spread + EPSILON) * gain

def rounded(values):
    return lax.optimization_barrier(values.astype(jnp.bfloat16)).astype(jnp.float32)

def finish(block, product, gains, weight_out, weight_gate):
    normed = rounded(layer_norm(block.astype(jnp.float32), gains[0]))
    gate = jax.nn.sigmoid(jnp.einsum('rnc,cd->rnd', normed, weight_gate.astype(jnp.float32)))
    scaled = rounded(layer_norm(product.astype(jnp.float32), gains[1]))
    update = jnp.einsum('rnc,cd->rnd', scaled, weight_out.astype(jnp.float32)) * gate
    return (block.astype(jnp.float32) + update).astype(jnp.bfloat16)

def triangle(pair, valid, gains, weight_in, weight_out, weight_gate, outward):
    total = pair.shape[0]
    width = weight_in.shape[0]
    if outward:
        picked = pair[:, ::3]
        mask_grid = valid[:, None] * valid[::3][None, :]
        step = ROWS_DEV
    else:
        picked = pair[::3]
        mask_grid = valid[::3][:, None] * valid[None, :]
        step = ROWS_DEV // 3

    def project_block(index):
        block = lax.dynamic_slice_in_dim(picked, index * step, step, 0)
        mask_block = lax.dynamic_slice_in_dim(mask_grid, index * step, step, 0)
        normed = rounded(layer_norm(block.astype(jnp.float32), gains[0]))
        hidden = jnp.einsum('rnc,cd->rnd', normed, weight_in.astype(jnp.float32))
        left = jax.nn.sigmoid(hidden[..., 2 * width:3 * width]) * hidden[..., :width] * mask_block[..., None]
        right = jax.nn.sigmoid(hidden[..., 3 * width:]) * hidden[..., width:2 * width] * mask_block[..., None]
        return (left.astype(jnp.bfloat16), right.astype(jnp.bfloat16))
    count = picked.shape[0] // step
    left, right = lax.map(project_block, jnp.arange(count, dtype=jnp.int32))
    left = left.reshape(picked.shape)
    right = right.reshape(picked.shape)
    left_major = jnp.transpose(left, (2, 0, 1)).astype(jnp.float32)
    right_major = jnp.transpose(right, (2, 0, 1)).astype(jnp.float32)

    def output_block(index):
        if outward:
            part = lax.dynamic_slice_in_dim(left_major, index * ROWS_DEV, ROWS_DEV, 1)
            product = jnp.einsum('cik,cjk->cij', part, right_major)
        else:
            part = lax.dynamic_slice_in_dim(left_major, index * ROWS_DEV, ROWS_DEV, 2)
            product = jnp.einsum('cki,ckj->cij', part, right_major)
        product = jnp.transpose(product.astype(jnp.bfloat16), (1, 2, 0))
        block = lax.dynamic_slice_in_dim(pair, index * ROWS_DEV, ROWS_DEV, 0)
        return finish(block, product, gains, weight_out, weight_gate)
    blocks = lax.map(output_block, jnp.arange(total // ROWS_DEV, dtype=jnp.int32))
    return blocks.reshape(pair.shape)

def reference(pair, pad_mask, token_count, norm_gain, proj_in, proj_out, gate_out):
    total = pair.shape[0]
    positions = jnp.arange(total, dtype=jnp.int32)
    valid = jnp.where((pad_mask > 0) & (positions < token_count[0]), 1.0, 0.0).astype(jnp.float32)
    first = triangle(pair, valid, norm_gain[0], proj_in[0], proj_out[0], gate_out[0], True)
    return triangle(first, valid, norm_gain[1], proj_in[1], proj_out[1], gate_out[1], False)
```

```python
import functools

import jax
import jax.numpy as jnp
from jax import lax
from jax.experimental import pallas as pl
from jax.experimental.pallas import tpu as pltpu
from jax.sharding import PartitionSpec as P

EPSILON = 1e-05
STEP = 3
TILE = 16
MESH = pl.DeviceIdType.MESH


def from_partner(value, axis, bit):
    mask = 2**bit
    pairs = [(source, source ^ mask) for source in range(lax.axis_size(axis))]
    return lax.ppermute(value, axis, pairs)


def layer_norm(values, gain):
    mean = jnp.mean(values, axis=-1, keepdims=True)
    centred = values - mean
    spread = jnp.mean(centred * centred, axis=-1, keepdims=True)
    return centred * lax.rsqrt(spread + EPSILON) * gain


def gated_pair(normed, weight, mask_grid):
    hidden = jnp.einsum("rnc,cd->rnd", normed, weight, preferred_element_type=jnp.float32)
    width = weight.shape[0]
    left = (
        jax.nn.sigmoid(hidden[..., 2 * width : 3 * width])
        * hidden[..., :width]
        * mask_grid[..., None]
    )
    right = (
        jax.nn.sigmoid(hidden[..., 3 * width :])
        * hidden[..., width : 2 * width]
        * mask_grid[..., None]
    )
    return (left.astype(jnp.bfloat16), right.astype(jnp.bfloat16))


def spread_out(left, right):
    moved = (
        lax.all_to_all(
            jnp.transpose(left, (2, 0, 1)), "row", split_axis=0, concat_axis=1, tiled=True
        ),
        lax.all_to_all(
            jnp.transpose(right, (2, 0, 1)), "row", split_axis=0, concat_axis=1, tiled=True
        ),
    )
    return (moved[0], moved[1])


def bring_back(product):
    moved = lax.all_to_all(product, "row", split_axis=1, concat_axis=0, tiled=True)
    return jnp.transpose(moved, (1, 2, 0))


def finish(pair, normed, product, gain_out, weight_out, weight_gate):
    gate = jax.nn.sigmoid(
        jnp.einsum("rnc,cd->rnd", normed, weight_gate, preferred_element_type=jnp.float32)
    )
    scaled = layer_norm(product.astype(jnp.float32), gain_out).astype(jnp.bfloat16)
    update = (
        jnp.einsum("rnc,cd->rnd", scaled, weight_out, preferred_element_type=jnp.float32) * gate
    )
    return (pair.astype(jnp.float32) + update).astype(jnp.bfloat16)


def outgoing(pair, row_valid, col_valid, gains, weight_in, weight_out, weight_gate):
    rows, width_cols, channels = pair.shape
    normed = layer_norm(pair.astype(jnp.float32), gains[0]).astype(jnp.bfloat16)
    picked = normed.reshape(rows, width_cols // 3, 3, channels)[:, :, 0]
    mask_grid = row_valid[:, None] * col_valid.reshape(width_cols // 3, 3)[:, 0][None, :]
    left, right = gated_pair(picked, weight_in, mask_grid)
    left, right = spread_out(left, right)
    col_index = lax.axis_index("col")
    full_left, every_right = (
        lax.all_gather(left, "col", axis=2, tiled=True),
        lax.all_gather(right, "col", axis=2, tiled=True),
    )
    full_right = lax.dynamic_slice_in_dim(every_right, col_index * width_cols, width_cols, 1)
    product = jnp.einsum("cik,cjk->cij", full_left, full_right, preferred_element_type=jnp.float32)
    product = bring_back(product.astype(jnp.bfloat16))
    return finish(pair, normed, product, gains[1], weight_out, weight_gate)


def incoming(pair, row_valid, col_valid, gains, weight_in, weight_out, weight_gate):
    rows, width_cols, channels = pair.shape
    normed = layer_norm(pair.astype(jnp.float32), gains[0]).astype(jnp.bfloat16)
    picked = normed.reshape(rows // 3, 3, width_cols, channels)[:, 0]
    mask_grid = row_valid.reshape(rows // 3, 3)[:, 0][:, None] * col_valid[None, :]
    left, right = gated_pair(picked, weight_in, mask_grid)
    left, right = spread_out(left, right)
    col_index = lax.axis_index("col")
    got = from_partner(left, "col", 0)
    full_left = jnp.where(
        col_index == 0, jnp.concatenate([left, got], axis=2), jnp.concatenate([got, left], axis=2)
    )
    product = jnp.einsum("cki,ckj->cij", full_left, right, preferred_element_type=jnp.float32)
    product = bring_back(product.astype(jnp.bfloat16))
    return finish(pair, normed, product, gains[1], weight_out, weight_gate)


def shards(pair, pad_mask, token_count, norm_gain, proj_in, proj_out, gate_out):
    rows, width_cols, channels = pair.shape
    total = pad_mask.shape[0]
    positions = jnp.arange(total, dtype=jnp.int32)
    valid = jnp.where((pad_mask > 0) & (positions < token_count[0]), 1.0, 0.0).astype(jnp.float32)
    row_valid = lax.dynamic_slice_in_dim(valid, lax.axis_index("row") * rows, rows)
    col_valid = lax.dynamic_slice_in_dim(valid, lax.axis_index("col") * width_cols, width_cols)
    first = outgoing(pair, row_valid, col_valid, norm_gain[0], proj_in[0], proj_out[0], gate_out[0])
    return incoming(first, row_valid, col_valid, norm_gain[1], proj_in[1], proj_out[1], gate_out[1])


def sigmoid(values):
    return 0.5 * jnp.tanh(0.5 * values) + 0.5


def narrow(values):
    return values.astype(jnp.bfloat16)


def rounded(values):
    return values.astype(jnp.bfloat16).astype(jnp.float32)


def dot(left, right):
    return jnp.dot(left, right, preferred_element_type=jnp.float32)


def iota(shape, axis):
    return lax.broadcasted_iota(jnp.int32, shape, axis)


def one_hot(index, width):
    return narrow(jnp.where(iota((index.shape[0], width), 1) == index, 1.0, 0.0))


def fused_kernel(
    rows_axis,
    width,
    pair_hbm,
    mask_hbm,
    count_hbm,
    gain_hbm,
    in_hbm,
    out_hbm,
    gate_hbm,
    result_ref,
    pair_v,
    mask_v,
    count_v,
    gain_v,
    in_v,
    out_v,
    gate_v,
    row_blocks,
    col_blocks,
    left_v,
    load_sem,
    send_row,
    recv_row,
    send_col,
    recv_col,
):
    channels = pair_v.shape[-1]
    total = STEP * rows_axis
    picks = width // STEP
    devices = 2 * rows_axis
    row = lax.axis_index("row")
    col = lax.axis_index("col")
    me = row * 2 + col
    half = row // picks
    own_slot = 2 * picks

    loads = [
        pltpu.make_async_copy(source, target, load_sem.at[at])
        for at, (source, target) in enumerate(
            [
                (pair_hbm, pair_v),
                (mask_hbm, mask_v),
                (count_hbm, count_v),
                (gain_hbm, gain_v),
                (in_hbm, in_v),
                (out_hbm, out_v),
                (gate_hbm, gate_v),
            ]
        )
    ]
    loads[0].start()

    col_blocks[...] = jnp.zeros_like(col_blocks)
    peers = []
    for offset in range(1, devices):
        peer = lax.rem(me + offset, devices)
        peers.append((peer, {"row": peer // 2, "col": lax.rem(peer, 2)}))
    barrier = pltpu.get_barrier_semaphore()
    for _, where in peers:
        pl.semaphore_signal(barrier, inc=1, device_id=where, device_id_type=MESH)
    for load in loads[1:]:
        load.start()

    loads[0].wait()
    pad = jnp.zeros((TILE - width, channels), jnp.float32)
    own = jnp.concatenate(
        [piece for t in range(STEP) for piece in (pair_v[t].astype(jnp.float32), pad)], axis=0
    )
    row_blocks[me] = narrow(own[:TILE])
    spot = iota((TILE, 1), 0)
    spot = jnp.where(spot < STEP * picks, spot // picks * TILE + spot % picks * STEP, -1)
    picked = narrow(dot(one_hot(spot, STEP * TILE), narrow(own)))
    col_blocks[own_slot + col] = picked

    @pl.when(col == half)
    def _():
        col_blocks[lax.rem(row, picks) * 2 + col] = picked

    pl.semaphore_wait(barrier, devices - 1)

    def row_copy(block, slot, where):
        return pltpu.make_async_remote_copy(
            src_ref=row_blocks.at[me],
            dst_ref=row_blocks.at[block],
            send_sem=send_row.at[slot],
            recv_sem=recv_row.at[block],
            device_id=where,
            device_id_type=MESH,
        )

    def col_copy(block, slot, where):
        return pltpu.make_async_remote_copy(
            src_ref=col_blocks.at[own_slot + col],
            dst_ref=col_blocks.at[block],
            send_sem=send_col.at[slot],
            recv_sem=recv_col.at[block],
            device_id=where,
            device_id_type=MESH,
        )

    sends = []
    my_slot = lax.rem(row, picks) * 2 + col
    sibling = {"row": row, "col": 1 - col}
    for at in range(devices - 1):
        copy = row_copy(me, at, peers[at][1])
        copy.start()
        sends.append(copy)
    for step in range(1, rows_axis):
        copy = col_copy(my_slot, step, {"row": lax.rem(row + step, rows_axis), "col": half})
        copy.start()
        sends.append(copy)
    copy = col_copy(own_slot + col, rows_axis, sibling)
    copy.start()
    sends.append(copy)
    extra = col_copy(my_slot, 0, sibling)

    @pl.when(col != half)
    def _():
        extra.start()

    def token_index(spot):
        inner = jnp.where(spot < width, col * width + spot, row * STEP + spot - width)
        return jnp.where(spot < width + STEP, inner, -1)

    summed = rows_axis
    n_left = summed * summed
    place = iota((n_left, 1), 0)
    a, k = place // summed, place % summed
    left_from = (a * 2 + k // picks) * TILE + k % picks * STEP
    place = iota((summed * TILE, 1), 0)
    a, j = place // TILE, place % TILE
    inside = jnp.where(
        j < width, (a * 2 + col) * TILE + j, (a * 2 + half) * TILE + STEP * (row % picks) + j - width
    )
    cross_from = jnp.where(j < width + STEP, inside, -1)
    select_rows = jnp.concatenate(
        [one_hot(left_from, devices * TILE), one_hot(cross_from, devices * TILE)], axis=0
    )
    slots = (own_slot + 2) * TILE
    place = iota((STEP * summed, 1), 0)
    t, k = place // summed, place % summed
    mine_from = (own_slot + k // picks) * TILE + t * picks + k % picks
    place = iota((summed * TILE, 1), 0)
    k, j = place // TILE, place % TILE
    inside = jnp.where(
        j < width,
        (j // STEP * 2 + k // picks) * TILE + j % STEP * picks + k % picks,
        (own_slot + k // picks) * TILE + (j - width) * picks + k % picks,
    )
    right_from = jnp.where(j < width + STEP, inside, -1)
    select_cols = jnp.concatenate([one_hot(mine_from, slots), one_hot(right_from, slots)], axis=0)

    for load in loads[1:4]:
        load.wait()
    lanes = iota((1, total), 1)
    valid = jnp.where((mask_v[...] > 0) & (lanes < count_v[...]), 1.0, 0.0)

    def pair_mask(first_index, second_index):
        grid = iota((first_index.shape[0], total), 1)
        both = jnp.where(grid == first_index, valid, 0.0) + jnp.where(
            grid == second_index, valid, 0.0
        )
        return jnp.where(jnp.sum(both, axis=-1, keepdims=True) > 1.5, 1.0, 0.0)

    place = iota(((summed + STEP) * summed, 1), 0)
    a, k = place // summed, place % summed
    left_mask = pair_mask(jnp.where(a < summed, STEP * a, row * STEP + a - summed), STEP * k)
    place = iota((summed * TILE, 1), 0)
    right_mask = pair_mask(token_index(place % TILE), STEP * (place // TILE))

    for load in loads[4:]:
        load.wait()

    for peer, where in peers:
        row_copy(peer, 0, where).wait_recv()
    for slot in range(own_slot):
        source = col * picks * 2 + slot

        @pl.when(source != me)
        def _():
            col_copy(slot, 0, sibling).wait_recv()

    col_copy(own_slot + 1 - col, 0, sibling).wait_recv()

    from_rows = dot(select_rows, row_blocks[...].reshape(devices * TILE, channels))
    from_cols = dot(select_cols, col_blocks[...].reshape(slots, channels))
    n_cross = summed * TILE
    block = jnp.concatenate([from_rows[n_left:], own], axis=0)
    normed = narrow(layer_norm(block, gain_v[0, 0][None]))
    side = jnp.concatenate([from_rows[:n_left], from_cols], axis=0)
    side = narrow(layer_norm(side, gain_v[0, 0][None]))
    n_side = n_left + STEP * summed
    gate = sigmoid(dot(normed, gate_v[0]))

    def gated(values, which, form, mask):
        value = dot(values, in_v[form, :, which * channels : (which + 1) * channels])
        opened = dot(values, in_v[form, :, (which + 2) * channels : (which + 3) * channels])
        return rounded(sigmoid(opened) * value * mask)

    left_v[0:n_side] = gated(side[:n_side], 0, 0, left_mask)
    right = gated(side[n_side:], 1, 0, right_mask)

    def finished(block, product, gate, form):
        scaled = narrow(layer_norm(rounded(product), gain_v[form, 1][None]))
        return rounded(block + dot(scaled, out_v[form]) * gate)

    def multiplied(row_of, count):
        products = []
        for a in range(count):
            acc = None
            for k in range(summed):
                at = row_of(a, k)
                term = left_v[at : at + 1] * right[k * TILE : (k + 1) * TILE]
                acc = term if acc is None else acc + term
            products.append(acc)
        return jnp.concatenate(products, axis=0)

    first = finished(block, multiplied(lambda a, k: a * summed + k, summed + STEP), gate, 0)

    normed = narrow(layer_norm(first, gain_v[1, 0][None]))
    gate = sigmoid(dot(normed[n_cross:], gate_v[1]))
    left_v[0:n_cross] = gated(normed[:n_cross], 0, 1, right_mask)
    right = gated(normed[:n_cross], 1, 1, right_mask)
    product = multiplied(lambda a, k: k * TILE + width + a, STEP)
    result = narrow(finished(first[n_cross:], product, gate, 1))
    for t in range(STEP):
        result_ref[t] = result[t * TILE : t * TILE + width]

    for copy in sends:
        copy.wait_send()

    @pl.when(col != half)
    def _():
        extra.wait_send()


def fused(pair, pad_mask, token_count, norm_gain, proj_in, proj_out, gate_out):
    rows, width, channels = pair.shape
    rows_axis = lax.axis_size("row")
    devices = 2 * rows_axis
    picks = width // STEP
    slots = 2 * picks + 2
    args = (
        pair,
        pad_mask.reshape(1, -1),
        token_count.reshape(1, 1),
        norm_gain,
        proj_in,
        proj_out,
        gate_out,
    )
    return pl.pallas_call(
        functools.partial(fused_kernel, rows_axis, width),
        out_shape=jax.ShapeDtypeStruct(pair.shape, pair.dtype),
        in_specs=[pl.BlockSpec(memory_space=pl.ANY)] * len(args),
        out_specs=pl.BlockSpec(memory_space=pltpu.VMEM),
        scratch_shapes=[pltpu.VMEM(arg.shape, arg.dtype) for arg in args]
        + [
            pltpu.VMEM((devices, TILE, channels), jnp.bfloat16),
            pltpu.VMEM((slots, TILE, channels), jnp.bfloat16),
            pltpu.VMEM((rows_axis * TILE, channels), jnp.float32),
            pltpu.SemaphoreType.DMA((len(args),)),
            pltpu.SemaphoreType.DMA((devices - 1,)),
            pltpu.SemaphoreType.DMA((devices,)),
            pltpu.SemaphoreType.DMA((rows_axis + 1,)),
            pltpu.SemaphoreType.DMA((slots,)),
        ],
        compiler_params=pltpu.CompilerParams(
            collective_id=0, has_side_effects=True, vmem_limit_bytes=32 * 1024 * 1024
        ),
        name="fused",
    )(*args)


def pick(mesh):
    def apply(pair, *rest):
        rows, width, _ = pair.shape
        rows_axis = mesh.shape["row"]
        small = (
            rows == STEP
            and mesh.shape["col"] == 2
            and 2 * width == STEP * rows_axis
            and width % STEP == 0
            and width + STEP <= TILE
        )
        return (fused if small else shards)(pair, *rest)

    return apply


def solution(mesh):
    in_specs = (P(("groups", "row"), "col", None), P("groups"), P("groups"), P(), P(), P(), P())
    out_specs = P(("groups", "row"), "col", None)
    return jax.shard_map(
        pick(mesh), mesh=mesh,
        in_specs=in_specs,
        out_specs=out_specs,
        check_vma=False,
    )
```

```python
import functools

import jax
import jax.numpy as jnp
from jax import lax
from jax.experimental import pallas as pl
from jax.experimental.pallas import tpu as pltpu
from jax.sharding import PartitionSpec as P

EPSILON = 1e-05
STEP = 3
TILE = 16
MESH = pl.DeviceIdType.MESH


def from_partner(value, axis, bit):
    mask = 2**bit
    pairs = [(source, source ^ mask) for source in range(lax.axis_size(axis))]
    return lax.ppermute(value, axis, pairs)


def layer_norm(values, gain):
    mean = jnp.mean(values, axis=-1, keepdims=True)
    centred = values - mean
    spread = jnp.mean(centred * centred, axis=-1, keepdims=True)
    return centred * lax.rsqrt(spread + EPSILON) * gain


def gated_pair(normed, weight, mask_grid):
    hidden = jnp.einsum("rnc,cd->rnd", normed, weight, preferred_element_type=jnp.float32)
    width = weight.shape[0]
    left = (
        jax.nn.sigmoid(hidden[..., 2 * width : 3 * width])
        * hidden[..., :width]
        * mask_grid[..., None]
    )
    right = (
        jax.nn.sigmoid(hidden[..., 3 * width :])
        * hidden[..., width : 2 * width]
        * mask_grid[..., None]
    )
    return (left.astype(jnp.bfloat16), right.astype(jnp.bfloat16))


def spread_out(left, right):
    moved = (
        lax.all_to_all(
            jnp.transpose(left, (2, 0, 1)), "row", split_axis=0, concat_axis=1, tiled=True
        ),
        lax.all_to_all(
            jnp.transpose(right, (2, 0, 1)), "row", split_axis=0, concat_axis=1, tiled=True
        ),
    )
    return (moved[0], moved[1])


def bring_back(product):
    moved = lax.all_to_all(product, "row", split_axis=1, concat_axis=0, tiled=True)
    return jnp.transpose(moved, (1, 2, 0))


def finish(pair, normed, product, gain_out, weight_out, weight_gate):
    gate = jax.nn.sigmoid(
        jnp.einsum("rnc,cd->rnd", normed, weight_gate, preferred_element_type=jnp.float32)
    )
    scaled = layer_norm(product.astype(jnp.float32), gain_out).astype(jnp.bfloat16)
    update = (
        jnp.einsum("rnc,cd->rnd", scaled, weight_out, preferred_element_type=jnp.float32) * gate
    )
    return (pair.astype(jnp.float32) + update).astype(jnp.bfloat16)


def outgoing(pair, row_valid, col_valid, gains, weight_in, weight_out, weight_gate):
    rows, width_cols, channels = pair.shape
    normed = layer_norm(pair.astype(jnp.float32), gains[0]).astype(jnp.bfloat16)
    picked = normed.reshape(rows, width_cols // 3, 3, channels)[:, :, 0]
    mask_grid = row_valid[:, None] * col_valid.reshape(width_cols // 3, 3)[:, 0][None, :]
    left, right = gated_pair(picked, weight_in, mask_grid)
    left, right = spread_out(left, right)
    col_index = lax.axis_index("col")
    full_left, every_right = (
        lax.all_gather(left, "col", axis=2, tiled=True),
        lax.all_gather(right, "col", axis=2, tiled=True),
    )
    full_right = lax.dynamic_slice_in_dim(every_right, col_index * width_cols, width_cols, 1)
    product = jnp.einsum("cik,cjk->cij", full_left, full_right, preferred_element_type=jnp.float32)
    product = bring_back(product.astype(jnp.bfloat16))
    return finish(pair, normed, product, gains[1], weight_out, weight_gate)


def incoming(pair, row_valid, col_valid, gains, weight_in, weight_out, weight_gate):
    rows, width_cols, channels = pair.shape
    normed = layer_norm(pair.astype(jnp.float32), gains[0]).astype(jnp.bfloat16)
    picked = normed.reshape(rows // 3, 3, width_cols, channels)[:, 0]
    mask_grid = row_valid.reshape(rows // 3, 3)[:, 0][:, None] * col_valid[None, :]
    left, right = gated_pair(picked, weight_in, mask_grid)
    left, right = spread_out(left, right)
    col_index = lax.axis_index("col")
    got = from_partner(left, "col", 0)
    full_left = jnp.where(
        col_index == 0, jnp.concatenate([left, got], axis=2), jnp.concatenate([got, left], axis=2)
    )
    product = jnp.einsum("cki,ckj->cij", full_left, right, preferred_element_type=jnp.float32)
    product = bring_back(product.astype(jnp.bfloat16))
    return finish(pair, normed, product, gains[1], weight_out, weight_gate)


def shards(pair, pad_mask, token_count, norm_gain, proj_in, proj_out, gate_out):
    rows, width_cols, channels = pair.shape
    total = pad_mask.shape[0]
    positions = jnp.arange(total, dtype=jnp.int32)
    valid = jnp.where((pad_mask > 0) & (positions < token_count[0]), 1.0, 0.0).astype(jnp.float32)
    row_valid = lax.dynamic_slice_in_dim(valid, lax.axis_index("row") * rows, rows)
    col_valid = lax.dynamic_slice_in_dim(valid, lax.axis_index("col") * width_cols, width_cols)
    first = outgoing(pair, row_valid, col_valid, norm_gain[0], proj_in[0], proj_out[0], gate_out[0])
    return incoming(first, row_valid, col_valid, norm_gain[1], proj_in[1], proj_out[1], gate_out[1])


def sigmoid(values):
    return 0.5 * jnp.tanh(0.5 * values) + 0.5


def narrow(values):
    return values.astype(jnp.bfloat16)


def rounded(values):
    return values.astype(jnp.bfloat16).astype(jnp.float32)


def dot(left, right):
    return jnp.dot(left, right, preferred_element_type=jnp.float32)


def iota(shape, axis):
    return lax.broadcasted_iota(jnp.int32, shape, axis)


def one_hot(index, width):
    return narrow(jnp.where(iota((index.shape[0], width), 1) == index, 1.0, 0.0))


def fused_kernel(
    rows_axis,
    width,
    pair_hbm,
    mask_hbm,
    count_hbm,
    gain_hbm,
    in_hbm,
    out_hbm,
    gate_hbm,
    result_ref,
    pair_v,
    mask_v,
    count_v,
    gain_v,
    in_v,
    out_v,
    gate_v,
    row_blocks,
    col_blocks,
    left_v,
    load_sem,
    send_row,
    recv_row,
    send_col,
    recv_col,
):
    channels = pair_v.shape[-1]
    total = STEP * rows_axis
    picks = width // STEP
    devices = 2 * rows_axis
    row = lax.axis_index("row")
    col = lax.axis_index("col")
    me = row * 2 + col
    half = row // picks
    own_slot = 2 * picks

    loads = [
        pltpu.make_async_copy(source, target, load_sem.at[at])
        for at, (source, target) in enumerate(
            [
                (pair_hbm, pair_v),
                (mask_hbm, mask_v),
                (count_hbm, count_v),
                (gain_hbm, gain_v),
                (in_hbm, in_v),
                (out_hbm, out_v),
                (gate_hbm, gate_v),
            ]
        )
    ]
    loads[0].start()

    col_blocks[...] = jnp.zeros_like(col_blocks)
    peers = []
    for offset in range(1, devices):
        peer = lax.rem(me + offset, devices)
        peers.append((peer, {"row": peer // 2, "col": lax.rem(peer, 2)}))
    barrier = pltpu.get_barrier_semaphore()
    for _, where in peers:
        pl.semaphore_signal(barrier, inc=1, device_id=where, device_id_type=MESH)
    for load in loads[1:]:
        load.start()

    loads[0].wait()
    pad = jnp.zeros((TILE - width, channels), jnp.float32)
    own = jnp.concatenate(
        [piece for t in range(STEP) for piece in (pair_v[t].astype(jnp.float32), pad)], axis=0
    )
    row_blocks[me] = narrow(own[:TILE])
    spot = iota((TILE, 1), 0)
    spot = jnp.where(spot < STEP * picks, spot // picks * TILE + spot % picks * STEP, -1)
    picked = narrow(dot(one_hot(spot, STEP * TILE), narrow(own)))
    col_blocks[own_slot + col] = picked

    @pl.when(col == half)
    def _():
        col_blocks[lax.rem(row, picks) * 2 + col] = picked

    pl.semaphore_wait(barrier, devices - 1)

    def row_copy(block, slot, where):
        return pltpu.make_async_remote_copy(
            src_ref=row_blocks.at[me],
            dst_ref=row_blocks.at[block],
            send_sem=send_row.at[slot],
            recv_sem=recv_row.at[block],
            device_id=where,
            device_id_type=MESH,
        )

    def col_copy(block, slot, where):
        return pltpu.make_async_remote_copy(
            src_ref=col_blocks.at[own_slot + col],
            dst_ref=col_blocks.at[block],
            send_sem=send_col.at[slot],
            recv_sem=recv_col.at[block],
            device_id=where,
            device_id_type=MESH,
        )

    sends = []
    my_slot = lax.rem(row, picks) * 2 + col
    sibling = {"row": row, "col": 1 - col}
    for at in range(devices - 1):
        copy = row_copy(me, at, peers[at][1])
        copy.start()
        sends.append(copy)
    for step in range(1, rows_axis):
        copy = col_copy(my_slot, step, {"row": lax.rem(row + step, rows_axis), "col": half})
        copy.start()
        sends.append(copy)
    copy = col_copy(own_slot + col, rows_axis, sibling)
    copy.start()
    sends.append(copy)
    extra = col_copy(my_slot, 0, sibling)

    @pl.when(col != half)
    def _():
        extra.start()

    def token_index(spot):
        inner = jnp.where(spot < width, col * width + spot, row * STEP + spot - width)
        return jnp.where(spot < width + STEP, inner, -1)

    summed = rows_axis
    n_left = summed * summed
    place = iota((n_left, 1), 0)
    a, k = place // summed, place % summed
    left_from = (a * 2 + k // picks) * TILE + k % picks * STEP
    place = iota((summed * TILE, 1), 0)
    a, j = place // TILE, place % TILE
    inside = jnp.where(
        j < width, (a * 2 + col) * TILE + j, (a * 2 + half) * TILE + STEP * (row % picks) + j - width
    )
    cross_from = jnp.where(j < width + STEP, inside, -1)
    select_rows = jnp.concatenate(
        [one_hot(left_from, devices * TILE), one_hot(cross_from, devices * TILE)], axis=0
    )
    slots = (own_slot + 2) * TILE
    place = iota((STEP * summed, 1), 0)
    t, k = place // summed, place % summed
    mine_from = (own_slot + k // picks) * TILE + t * picks + k % picks
    place = iota((summed * TILE, 1), 0)
    k, j = place // TILE, place % TILE
    inside = jnp.where(
        j < width,
        (j // STEP * 2 + k // picks) * TILE + j % STEP * picks + k % picks,
        (own_slot + k // picks) * TILE + (j - width) * picks + k % picks,
    )
    right_from = jnp.where(j < width + STEP, inside, -1)
    select_cols = jnp.concatenate([one_hot(mine_from, slots), one_hot(right_from, slots)], axis=0)

    for load in loads[1:4]:
        load.wait()
    lanes = iota((1, total), 1)
    valid = jnp.where((mask_v[...] > 0) & (lanes < count_v[...]), 1.0, 0.0)

    def pair_mask(first_index, second_index):
        grid = iota((first_index.shape[0], total), 1)
        both = jnp.where(grid == first_index, valid, 0.0) + jnp.where(
            grid == second_index, valid, 0.0
        )
        return jnp.where(jnp.sum(both, axis=-1, keepdims=True) > 1.5, 1.0, 0.0)

    place = iota(((summed + STEP) * summed, 1), 0)
    a, k = place // summed, place % summed
    left_mask = pair_mask(jnp.where(a < summed, STEP * a, row * STEP + a - summed), STEP * k)
    place = iota((summed * TILE, 1), 0)
    right_mask = pair_mask(token_index(place % TILE), STEP * (place // TILE))

    for load in loads[4:]:
        load.wait()

    for peer, where in peers:
        row_copy(peer, 0, where).wait_recv()
    for slot in range(own_slot):
        source = col * picks * 2 + slot

        @pl.when(source != me)
        def _():
            col_copy(slot, 0, sibling).wait_recv()

    col_copy(own_slot + 1 - col, 0, sibling).wait_recv()

    from_rows = dot(select_rows, row_blocks[...].reshape(devices * TILE, channels))
    from_cols = dot(select_cols, col_blocks[...].reshape(slots, channels))
    n_cross = summed * TILE
    block = jnp.concatenate([from_rows[n_left:], own], axis=0)
    normed = narrow(layer_norm(block, gain_v[0, 0][None]))
    side = jnp.concatenate([from_rows[:n_left], from_cols], axis=0)
    side = narrow(layer_norm(side, gain_v[0, 0][None]))
    n_side = n_left + STEP * summed
    gate = sigmoid(dot(normed, gate_v[0]))

    def gated(values, which, form, mask):
        value = dot(values, in_v[form, :, which * channels : (which + 1) * channels])
        opened = dot(values, in_v[form, :, (which + 2) * channels : (which + 3) * channels])
        return rounded(sigmoid(opened) * value * mask)

    left_v[0:n_side] = gated(side[:n_side], 0, 0, left_mask)
    right = gated(side[n_side:], 1, 0, right_mask)

    def finished(block, product, gate, form):
        scaled = narrow(layer_norm(rounded(product), gain_v[form, 1][None]))
        return rounded(block + dot(scaled, out_v[form]) * gate)

    def multiplied(row_of, count):
        products = []
        for a in range(count):
            acc = None
            for k in range(summed):
                at = row_of(a, k)
                term = left_v[at : at + 1] * right[k * TILE : (k + 1) * TILE]
                acc = term if acc is None else acc + term
            products.append(acc)
        return jnp.concatenate(products, axis=0)

    first = finished(block, multiplied(lambda a, k: a * summed + k, summed + STEP), gate, 0)

    normed = narrow(layer_norm(first, gain_v[1, 0][None]))
    gate = sigmoid(dot(normed[n_cross:], gate_v[1]))
    left_v[0:n_cross] = gated(normed[:n_cross], 0, 1, right_mask)
    right = gated(normed[:n_cross], 1, 1, right_mask)
    product = multiplied(lambda a, k: k * TILE + width + a, STEP)
    result = narrow(finished(first[n_cross:], product, gate, 1))
    for t in range(STEP):
        result_ref[t] = result[t * TILE : t * TILE + width]

    for copy in sends:
        copy.wait_send()

    @pl.when(col != half)
    def _():
        extra.wait_send()


def fused(pair, pad_mask, token_count, norm_gain, proj_in, proj_out, gate_out):
    rows, width, channels = pair.shape
    rows_axis = lax.axis_size("row")
    devices = 2 * rows_axis
    picks = width // STEP
    slots = 2 * picks + 2
    args = (
        pair,
        pad_mask.reshape(1, -1),
        token_count.reshape(1, 1),
        norm_gain,
        proj_in,
        proj_out,
        gate_out,
    )
    return pl.pallas_call(
        functools.partial(fused_kernel, rows_axis, width),
        out_shape=jax.ShapeDtypeStruct(pair.shape, pair.dtype),
        in_specs=[pl.BlockSpec(memory_space=pltpu.HBM)] * len(args),
        out_specs=pl.BlockSpec(memory_space=pltpu.VMEM),
        scratch_shapes=[pltpu.VMEM(arg.shape, arg.dtype) for arg in args]
        + [
            pltpu.VMEM((devices, TILE, channels), jnp.bfloat16),
            pltpu.VMEM((slots, TILE, channels), jnp.bfloat16),
            pltpu.VMEM((rows_axis * TILE, channels), jnp.float32),
            pltpu.SemaphoreType.DMA((len(args),)),
            pltpu.SemaphoreType.DMA((devices - 1,)),
            pltpu.SemaphoreType.DMA((devices,)),
            pltpu.SemaphoreType.DMA((rows_axis + 1,)),
            pltpu.SemaphoreType.DMA((slots,)),
        ],
        compiler_params=pltpu.CompilerParams(
            collective_id=0, has_side_effects=True, vmem_limit_bytes=32 * 1024 * 1024
        ),
        name="fused",
    )(*args)


def pick(mesh):
    def apply(pair, *rest):
        rows, width, _ = pair.shape
        rows_axis = mesh.shape["row"]
        small = (
            rows == STEP
            and mesh.shape["col"] == 2
            and 2 * width == STEP * rows_axis
            and width % STEP == 0
            and width + STEP <= TILE
        )
        return (fused if small else shards)(pair, *rest)

    return apply


def solution(mesh):
    in_specs = (P(("groups", "row"), "col", None), P("groups"), P("groups"), P(), P(), P(), P())
    out_specs = P(("groups", "row"), "col", None)
    return jax.shard_map(
        pick(mesh),
        mesh=mesh,
        in_specs=in_specs,
        out_specs=out_specs,
        check_vma=False,
    )
```

```python
import functools

import jax
import jax.numpy as jnp
from jax import lax
from jax.experimental import pallas as pl
from jax.experimental.pallas import tpu as pltpu
from jax.sharding import PartitionSpec as P

EPSILON = 1e-05
STEP = 3
TILE = 16
MESH = pl.DeviceIdType.MESH


def from_partner(value, axis, bit):
    mask = 2**bit
    pairs = [(source, source ^ mask) for source in range(lax.axis_size(axis))]
    return lax.ppermute(value, axis, pairs)


def layer_norm(values, gain):
    mean = jnp.mean(values, axis=-1, keepdims=True)
    centred = values - mean
    spread = jnp.mean(centred * centred, axis=-1, keepdims=True)
    return centred * lax.rsqrt(spread + EPSILON) * gain


def gated_pair(normed, weight, mask_grid):
    hidden = jnp.einsum("rnc,cd->rnd", normed, weight, preferred_element_type=jnp.float32)
    width = weight.shape[0]
    left = (
        jax.nn.sigmoid(hidden[..., 2 * width : 3 * width])
        * hidden[..., :width]
        * mask_grid[..., None]
    )
    right = (
        jax.nn.sigmoid(hidden[..., 3 * width :])
        * hidden[..., width : 2 * width]
        * mask_grid[..., None]
    )
    return (left.astype(jnp.bfloat16), right.astype(jnp.bfloat16))


def spread_out(left, right):
    moved = (
        lax.all_to_all(
            jnp.transpose(left, (2, 0, 1)), "row", split_axis=0, concat_axis=1, tiled=True
        ),
        lax.all_to_all(
            jnp.transpose(right, (2, 0, 1)), "row", split_axis=0, concat_axis=1, tiled=True
        ),
    )
    return (moved[0], moved[1])


def bring_back(product):
    moved = lax.all_to_all(product, "row", split_axis=1, concat_axis=0, tiled=True)
    return jnp.transpose(moved, (1, 2, 0))


def finish(pair, normed, product, gain_out, weight_out, weight_gate):
    gate = jax.nn.sigmoid(
        jnp.einsum("rnc,cd->rnd", normed, weight_gate, preferred_element_type=jnp.float32)
    )
    scaled = layer_norm(product.astype(jnp.float32), gain_out).astype(jnp.bfloat16)
    update = (
        jnp.einsum("rnc,cd->rnd", scaled, weight_out, preferred_element_type=jnp.float32) * gate
    )
    return (pair.astype(jnp.float32) + update).astype(jnp.bfloat16)


def outgoing(pair, row_valid, col_valid, gains, weight_in, weight_out, weight_gate):
    rows, width_cols, channels = pair.shape
    normed = layer_norm(pair.astype(jnp.float32), gains[0]).astype(jnp.bfloat16)
    picked = normed.reshape(rows, width_cols // 3, 3, channels)[:, :, 0]
    mask_grid = row_valid[:, None] * col_valid.reshape(width_cols // 3, 3)[:, 0][None, :]
    left, right = gated_pair(picked, weight_in, mask_grid)
    left, right = spread_out(left, right)
    col_index = lax.axis_index("col")
    full_left, every_right = (
        lax.all_gather(left, "col", axis=2, tiled=True),
        lax.all_gather(right, "col", axis=2, tiled=True),
    )
    full_right = lax.dynamic_slice_in_dim(every_right, col_index * width_cols, width_cols, 1)
    product = jnp.einsum("cik,cjk->cij", full_left, full_right, preferred_element_type=jnp.float32)
    product = bring_back(product.astype(jnp.bfloat16))
    return finish(pair, normed, product, gains[1], weight_out, weight_gate)


def incoming(pair, row_valid, col_valid, gains, weight_in, weight_out, weight_gate):
    rows, width_cols, channels = pair.shape
    normed = layer_norm(pair.astype(jnp.float32), gains[0]).astype(jnp.bfloat16)
    picked = normed.reshape(rows // 3, 3, width_cols, channels)[:, 0]
    mask_grid = row_valid.reshape(rows // 3, 3)[:, 0][:, None] * col_valid[None, :]
    left, right = gated_pair(picked, weight_in, mask_grid)
    left, right = spread_out(left, right)
    col_index = lax.axis_index("col")
    got = from_partner(left, "col", 0)
    full_left = jnp.where(
        col_index == 0, jnp.concatenate([left, got], axis=2), jnp.concatenate([got, left], axis=2)
    )
    product = jnp.einsum("cki,ckj->cij", full_left, right, preferred_element_type=jnp.float32)
    product = bring_back(product.astype(jnp.bfloat16))
    return finish(pair, normed, product, gains[1], weight_out, weight_gate)


def shards(pair, pad_mask, token_count, norm_gain, proj_in, proj_out, gate_out):
    rows, width_cols, channels = pair.shape
    total = pad_mask.shape[0]
    positions = jnp.arange(total, dtype=jnp.int32)
    valid = jnp.where((pad_mask > 0) & (positions < token_count[0]), 1.0, 0.0).astype(jnp.float32)
    row_valid = lax.dynamic_slice_in_dim(valid, lax.axis_index("row") * rows, rows)
    col_valid = lax.dynamic_slice_in_dim(valid, lax.axis_index("col") * width_cols, width_cols)
    first = outgoing(pair, row_valid, col_valid, norm_gain[0], proj_in[0], proj_out[0], gate_out[0])
    return incoming(first, row_valid, col_valid, norm_gain[1], proj_in[1], proj_out[1], gate_out[1])


def sigmoid(values):
    return 0.5 * jnp.tanh(0.5 * values) + 0.5


def narrow(values):
    return values.astype(jnp.bfloat16)


def rounded(values):
    return values.astype(jnp.bfloat16).astype(jnp.float32)


def dot(left, right):
    return jnp.dot(left, right, preferred_element_type=jnp.float32)


def iota(shape, axis):
    return lax.broadcasted_iota(jnp.int32, shape, axis)


def one_hot(index, width):
    return narrow(jnp.where(iota((index.shape[0], width), 1) == index, 1.0, 0.0))


def fused_kernel(
    rows_axis,
    width,
    pair_hbm,
    mask_hbm,
    count_hbm,
    gain_hbm,
    in_hbm,
    out_hbm,
    gate_hbm,
    result_ref,
    pair_v,
    mask_v,
    count_v,
    gain_v,
    in_v,
    out_v,
    gate_v,
    row_blocks,
    col_blocks,
    left_v,
    load_sem,
    send_row,
    recv_row,
    send_col,
    recv_col,
):
    channels = pair_v.shape[-1]
    total = STEP * rows_axis
    picks = width // STEP
    devices = 2 * rows_axis
    row = lax.axis_index("row")
    col = lax.axis_index("col")
    me = row * 2 + col
    half = row // picks
    own_slot = 2 * picks

    loads = [
        pltpu.make_async_copy(source, target, load_sem.at[at])
        for at, (source, target) in enumerate(
            [
                (pair_hbm, pair_v),
                (mask_hbm, mask_v),
                (count_hbm, count_v),
                (gain_hbm, gain_v),
                (in_hbm, in_v),
                (out_hbm, out_v),
                (gate_hbm, gate_v),
            ]
        )
    ]
    loads[0].start()

    col_blocks[...] = jnp.zeros_like(col_blocks)
    peers = []
    for offset in range(1, devices):
        peer = lax.rem(me + offset, devices)
        peers.append((peer, {"row": peer // 2, "col": lax.rem(peer, 2)}))
    barrier = pltpu.get_barrier_semaphore()
    for _, where in peers:
        pl.semaphore_signal(barrier, inc=1, device_id=where, device_id_type=MESH)
    for load in loads[1:]:
        load.start()

    loads[0].wait()
    pad = jnp.zeros((TILE - width, channels), jnp.float32)
    own = jnp.concatenate(
        [piece for t in range(STEP) for piece in (pair_v[t].astype(jnp.float32), pad)], axis=0
    )
    row_blocks[me] = narrow(own[:TILE])
    spot = iota((TILE, 1), 0)
    spot = jnp.where(spot < STEP * picks, spot // picks * TILE + spot % picks * STEP, -1)
    picked = narrow(dot(one_hot(spot, STEP * TILE), narrow(own)))
    col_blocks[own_slot + col] = picked

    @pl.when(col == half)
    def _():
        col_blocks[lax.rem(row, picks) * 2 + col] = picked

    pl.semaphore_wait(barrier, devices - 1)

    def row_copy(block, slot, where):
        return pltpu.make_async_remote_copy(
            src_ref=row_blocks.at[me],
            dst_ref=row_blocks.at[block],
            send_sem=send_row.at[slot],
            recv_sem=recv_row.at[block],
            device_id=where,
            device_id_type=MESH,
        )

    def col_copy(block, slot, where):
        return pltpu.make_async_remote_copy(
            src_ref=col_blocks.at[own_slot + col],
            dst_ref=col_blocks.at[block],
            send_sem=send_col.at[slot],
            recv_sem=recv_col.at[block],
            device_id=where,
            device_id_type=MESH,
        )

    sends = []
    my_slot = lax.rem(row, picks) * 2 + col
    sibling = {"row": row, "col": 1 - col}
    for at in range(devices - 1):
        copy = row_copy(me, at, peers[at][1])
        copy.start()
        sends.append(copy)
    for step in range(1, rows_axis):
        copy = col_copy(my_slot, step, {"row": lax.rem(row + step, rows_axis), "col": half})
        copy.start()
        sends.append(copy)
    copy = col_copy(own_slot + col, rows_axis, sibling)
    copy.start()
    sends.append(copy)
    extra = col_copy(my_slot, 0, sibling)

    @pl.when(col != half)
    def _():
        extra.start()

    def token_index(spot):
        inner = jnp.where(spot < width, col * width + spot, row * STEP + spot - width)
        return jnp.where(spot < width + STEP, inner, -1)

    summed = rows_axis
    n_left = summed * summed
    place = iota((n_left, 1), 0)
    a, k = place // summed, place % summed
    left_from = (a * 2 + k // picks) * TILE + k % picks * STEP
    place = iota((summed * TILE, 1), 0)
    a, j = place // TILE, place % TILE
    inside = jnp.where(
        j < width, (a * 2 + col) * TILE + j, (a * 2 + half) * TILE + STEP * (row % picks) + j - width
    )
    cross_from = jnp.where(j < width + STEP, inside, -1)
    select_rows = jnp.concatenate(
        [one_hot(left_from, devices * TILE), one_hot(cross_from, devices * TILE)], axis=0
    )
    slots = (own_slot + 2) * TILE
    place = iota((STEP * summed, 1), 0)
    t, k = place // summed, place % summed
    mine_from = (own_slot + k // picks) * TILE + t * picks + k % picks
    place = iota((summed * TILE, 1), 0)
    k, j = place // TILE, place % TILE
    inside = jnp.where(
        j < width,
        (j // STEP * 2 + k // picks) * TILE + j % STEP * picks + k % picks,
        (own_slot + k // picks) * TILE + (j - width) * picks + k % picks,
    )
    right_from = jnp.where(j < width + STEP, inside, -1)
    select_cols = jnp.concatenate([one_hot(mine_from, slots), one_hot(right_from, slots)], axis=0)

    for load in loads[1:4]:
        load.wait()
    lanes = iota((1, total), 1)
    valid = jnp.where((mask_v[...] > 0) & (lanes < count_v[0]), 1.0, 0.0)

    def pair_mask(first_index, second_index):
        grid = iota((first_index.shape[0], total), 1)
        both = jnp.where(grid == first_index, valid, 0.0) + jnp.where(
            grid == second_index, valid, 0.0
        )
        return jnp.where(jnp.sum(both, axis=-1, keepdims=True) > 1.5, 1.0, 0.0)

    place = iota(((summed + STEP) * summed, 1), 0)
    a, k = place // summed, place % summed
    left_mask = pair_mask(jnp.where(a < summed, STEP * a, row * STEP + a - summed), STEP * k)
    place = iota((summed * TILE, 1), 0)
    right_mask = pair_mask(token_index(place % TILE), STEP * (place // TILE))

    for load in loads[4:]:
        load.wait()

    for peer, where in peers:
        row_copy(peer, 0, where).wait_recv()
    for slot in range(own_slot):
        source = col * picks * 2 + slot

        @pl.when(source != me)
        def _():
            col_copy(slot, 0, sibling).wait_recv()

    col_copy(own_slot + 1 - col, 0, sibling).wait_recv()

    from_rows = dot(select_rows, row_blocks[...].reshape(devices * TILE, channels))
    from_cols = dot(select_cols, col_blocks[...].reshape(slots, channels))
    n_cross = summed * TILE
    block = jnp.concatenate([from_rows[n_left:], own], axis=0)
    normed = narrow(layer_norm(block, gain_v[0, 0][None]))
    side = jnp.concatenate([from_rows[:n_left], from_cols], axis=0)
    side = narrow(layer_norm(side, gain_v[0, 0][None]))
    n_side = n_left + STEP * summed
    gate = sigmoid(dot(normed, gate_v[0]))

    def gated(values, which, form, mask):
        value = dot(values, in_v[form, :, which * channels : (which + 1) * channels])
        opened = dot(values, in_v[form, :, (which + 2) * channels : (which + 3) * channels])
        return rounded(sigmoid(opened) * value * mask)

    left_v[0:n_side] = gated(side[:n_side], 0, 0, left_mask)
    right = gated(side[n_side:], 1, 0, right_mask)

    def finished(block, product, gate, form):
        scaled = narrow(layer_norm(rounded(product), gain_v[form, 1][None]))
        return rounded(block + dot(scaled, out_v[form]) * gate)

    def multiplied(row_of, count):
        products = []
        for a in range(count):
            acc = None
            for k in range(summed):
                at = row_of(a, k)
                term = left_v[at : at + 1] * right[k * TILE : (k + 1) * TILE]
                acc = term if acc is None else acc + term
            products.append(acc)
        return jnp.concatenate(products, axis=0)

    first = finished(block, multiplied(lambda a, k: a * summed + k, summed + STEP), gate, 0)

    normed = narrow(layer_norm(first, gain_v[1, 0][None]))
    gate = sigmoid(dot(normed[n_cross:], gate_v[1]))
    left_v[0:n_cross] = gated(normed[:n_cross], 0, 1, right_mask)
    right = gated(normed[:n_cross], 1, 1, right_mask)
    product = multiplied(lambda a, k: k * TILE + width + a, STEP)
    result = narrow(finished(first[n_cross:], product, gate, 1))
    for t in range(STEP):
        result_ref[t] = result[t * TILE : t * TILE + width]

    for copy in sends:
        copy.wait_send()

    @pl.when(col != half)
    def _():
        extra.wait_send()


def fused(pair, pad_mask, token_count, norm_gain, proj_in, proj_out, gate_out):
    rows, width, channels = pair.shape
    rows_axis = lax.axis_size("row")
    devices = 2 * rows_axis
    picks = width // STEP
    slots = 2 * picks + 2
    args = (
        pair,
        pad_mask.reshape(1, -1),
        token_count,
        norm_gain,
        proj_in,
        proj_out,
        gate_out,
    )
    return pl.pallas_call(
        functools.partial(fused_kernel, rows_axis, width),
        out_shape=jax.ShapeDtypeStruct(pair.shape, pair.dtype),
        in_specs=[pl.BlockSpec(memory_space=pl.ANY)] * len(args),
        out_specs=pl.BlockSpec(memory_space=pltpu.VMEM),
        scratch_shapes=[
            (pltpu.SMEM if arg is token_count else pltpu.VMEM)(arg.shape, arg.dtype) for arg in args
        ]
        + [
            pltpu.VMEM((devices, TILE, channels), jnp.bfloat16),
            pltpu.VMEM((slots, TILE, channels), jnp.bfloat16),
            pltpu.VMEM((rows_axis * TILE, channels), jnp.float32),
            pltpu.SemaphoreType.DMA((len(args),)),
            pltpu.SemaphoreType.DMA((devices - 1,)),
            pltpu.SemaphoreType.DMA((devices,)),
            pltpu.SemaphoreType.DMA((rows_axis + 1,)),
            pltpu.SemaphoreType.DMA((slots,)),
        ],
        compiler_params=pltpu.CompilerParams(
            collective_id=0, has_side_effects=True, vmem_limit_bytes=56 * 1024 * 1024
        ),
        name="fused",
    )(*args)


def pick(mesh):
    def apply(pair, *rest):
        rows, width, _ = pair.shape
        rows_axis = mesh.shape["row"]
        small = (
            rows == STEP
            and mesh.shape["col"] == 2
            and 2 * width == STEP * rows_axis
            and width % STEP == 0
            and width + STEP <= TILE
        )
        return (fused if small else shards)(pair, *rest)

    return apply


def solution(mesh):
    in_specs = (P(("groups", "row"), "col", None), P("groups"), P("groups"), P(), P(), P(), P())
    out_specs = P(("groups", "row"), "col", None)
    return jax.shard_map(
        pick(mesh),
        mesh=mesh,
        in_specs=in_specs,
        out_specs=out_specs,
        check_vma=False,
    )
```

```python
import functools

import jax
import jax.numpy as jnp
from jax import lax
from jax.experimental import pallas as pl
from jax.experimental.pallas import tpu as pltpu
from jax.sharding import PartitionSpec as P

EPSILON = 1e-05
STEP = 3
TILE = 16
MESH = pl.DeviceIdType.MESH


def from_partner(value, axis, bit):
    mask = 2**bit
    pairs = [(source, source ^ mask) for source in range(lax.axis_size(axis))]
    return lax.ppermute(value, axis, pairs)


def layer_norm(values, gain):
    mean = jnp.mean(values, axis=-1, keepdims=True)
    centred = values - mean
    spread = jnp.mean(centred * centred, axis=-1, keepdims=True)
    return centred * lax.rsqrt(spread + EPSILON) * gain


def gated_pair(normed, weight, mask_grid):
    hidden = jnp.einsum("rnc,cd->rnd", normed, weight, preferred_element_type=jnp.float32)
    width = weight.shape[0]
    left = (
        jax.nn.sigmoid(hidden[..., 2 * width : 3 * width])
        * hidden[..., :width]
        * mask_grid[..., None]
    )
    right = (
        jax.nn.sigmoid(hidden[..., 3 * width :])
        * hidden[..., width : 2 * width]
        * mask_grid[..., None]
    )
    return (left.astype(jnp.bfloat16), right.astype(jnp.bfloat16))


def spread_out(left, right):
    moved = (
        lax.all_to_all(
            jnp.transpose(left, (2, 0, 1)), "row", split_axis=0, concat_axis=1, tiled=True
        ),
        lax.all_to_all(
            jnp.transpose(right, (2, 0, 1)), "row", split_axis=0, concat_axis=1, tiled=True
        ),
    )
    return (moved[0], moved[1])


def bring_back(product):
    moved = lax.all_to_all(product, "row", split_axis=1, concat_axis=0, tiled=True)
    return jnp.transpose(moved, (1, 2, 0))


def finish(pair, normed, product, gain_out, weight_out, weight_gate):
    gate = jax.nn.sigmoid(
        jnp.einsum("rnc,cd->rnd", normed, weight_gate, preferred_element_type=jnp.float32)
    )
    scaled = layer_norm(product.astype(jnp.float32), gain_out).astype(jnp.bfloat16)
    update = (
        jnp.einsum("rnc,cd->rnd", scaled, weight_out, preferred_element_type=jnp.float32) * gate
    )
    return (pair.astype(jnp.float32) + update).astype(jnp.bfloat16)


def outgoing(pair, row_valid, col_valid, gains, weight_in, weight_out, weight_gate):
    rows, width_cols, channels = pair.shape
    normed = layer_norm(pair.astype(jnp.float32), gains[0]).astype(jnp.bfloat16)
    picked = normed.reshape(rows, width_cols // 3, 3, channels)[:, :, 0]
    mask_grid = row_valid[:, None] * col_valid.reshape(width_cols // 3, 3)[:, 0][None, :]
    left, right = gated_pair(picked, weight_in, mask_grid)
    left, right = spread_out(left, right)
    col_index = lax.axis_index("col")
    full_left, every_right = (
        lax.all_gather(left, "col", axis=2, tiled=True),
        lax.all_gather(right, "col", axis=2, tiled=True),
    )
    full_right = lax.dynamic_slice_in_dim(every_right, col_index * width_cols, width_cols, 1)
    product = jnp.einsum("cik,cjk->cij", full_left, full_right, preferred_element_type=jnp.float32)
    product = bring_back(product.astype(jnp.bfloat16))
    return finish(pair, normed, product, gains[1], weight_out, weight_gate)


def incoming(pair, row_valid, col_valid, gains, weight_in, weight_out, weight_gate):
    rows, width_cols, channels = pair.shape
    normed = layer_norm(pair.astype(jnp.float32), gains[0]).astype(jnp.bfloat16)
    picked = normed.reshape(rows // 3, 3, width_cols, channels)[:, 0]
    mask_grid = row_valid.reshape(rows // 3, 3)[:, 0][:, None] * col_valid[None, :]
    left, right = gated_pair(picked, weight_in, mask_grid)
    left, right = spread_out(left, right)
    col_index = lax.axis_index("col")
    got = from_partner(left, "col", 0)
    full_left = jnp.where(
        col_index == 0, jnp.concatenate([left, got], axis=2), jnp.concatenate([got, left], axis=2)
    )
    product = jnp.einsum("cki,ckj->cij", full_left, right, preferred_element_type=jnp.float32)
    product = bring_back(product.astype(jnp.bfloat16))
    return finish(pair, normed, product, gains[1], weight_out, weight_gate)


def shards(pair, pad_mask, token_count, norm_gain, proj_in, proj_out, gate_out):
    rows, width_cols, channels = pair.shape
    total = pad_mask.shape[0]
    positions = jnp.arange(total, dtype=jnp.int32)
    valid = jnp.where((pad_mask > 0) & (positions < token_count[0]), 1.0, 0.0).astype(jnp.float32)
    row_valid = lax.dynamic_slice_in_dim(valid, lax.axis_index("row") * rows, rows)
    col_valid = lax.dynamic_slice_in_dim(valid, lax.axis_index("col") * width_cols, width_cols)
    first = outgoing(pair, row_valid, col_valid, norm_gain[0], proj_in[0], proj_out[0], gate_out[0])
    return incoming(first, row_valid, col_valid, norm_gain[1], proj_in[1], proj_out[1], gate_out[1])


def sigmoid(values):
    return 0.5 * jnp.tanh(0.5 * values) + 0.5


def narrow(values):
    return values.astype(jnp.bfloat16)


def rounded(values):
    return values.astype(jnp.bfloat16).astype(jnp.float32)


def dot(left, right):
    return jnp.dot(left, right, preferred_element_type=jnp.float32)


def iota(shape, axis):
    return lax.broadcasted_iota(jnp.int32, shape, axis)


def one_hot(index, width):
    return narrow(jnp.where(iota((index.shape[0], width), 1) == index, 1.0, 0.0))


def fused_kernel(
    rows_axis,
    width,
    pair_hbm,
    mask_hbm,
    count_hbm,
    gain_hbm,
    in_hbm,
    out_hbm,
    gate_hbm,
    result_ref,
    pair_v,
    mask_v,
    count_v,
    gain_v,
    in_v,
    out_v,
    gate_v,
    row_blocks,
    col_blocks,
    left_v,
    load_sem,
    send_row,
    recv_row,
    send_col,
    recv_col,
):
    channels = pair_v.shape[-1]
    total = STEP * rows_axis
    picks = width // STEP
    devices = 2 * rows_axis
    row = lax.axis_index("row")
    col = lax.axis_index("col")
    me = row * 2 + col
    half = row // picks
    own_slot = 2 * picks

    loads = [
        pltpu.make_async_copy(source, target, load_sem.at[at])
        for at, (source, target) in enumerate(
            [
                (pair_hbm, pair_v),
                (mask_hbm, mask_v),
                (count_hbm, count_v),
                (gain_hbm, gain_v),
                (in_hbm, in_v),
                (out_hbm, out_v),
                (gate_hbm, gate_v),
            ]
        )
    ]
    loads[0].start()

    col_blocks[...] = jnp.zeros_like(col_blocks)
    peers = []
    for offset in range(1, devices):
        peer = lax.rem(me + offset, devices)
        peers.append((peer, {"row": peer // 2, "col": lax.rem(peer, 2)}))
    barrier = pltpu.get_barrier_semaphore()
    for _, where in peers:
        pl.semaphore_signal(barrier, inc=1, device_id=where, device_id_type=MESH)
    for load in loads[1:]:
        load.start()

    loads[0].wait()
    pad = jnp.zeros((TILE - width, channels), jnp.float32)
    own = jnp.concatenate(
        [piece for t in range(STEP) for piece in (pair_v[t].astype(jnp.float32), pad)], axis=0
    )
    row_blocks[me] = narrow(own[:TILE])
    pl.semaphore_wait(barrier, devices - 1)

    def row_copy(block, slot, where):
        return pltpu.make_async_remote_copy(
            src_ref=row_blocks.at[me],
            dst_ref=row_blocks.at[block],
            send_sem=send_row.at[slot],
            recv_sem=recv_row.at[block],
            device_id=where,
            device_id_type=MESH,
        )

    def col_copy(block, slot, where):
        return pltpu.make_async_remote_copy(
            src_ref=col_blocks.at[own_slot + col],
            dst_ref=col_blocks.at[block],
            send_sem=send_col.at[slot],
            recv_sem=recv_col.at[block],
            device_id=where,
            device_id_type=MESH,
        )

    sends = []
    my_slot = lax.rem(row, picks) * 2 + col
    sibling = {"row": row, "col": 1 - col}
    for at in range(devices - 1):
        copy = row_copy(me, at, peers[at][1])
        copy.start()
        sends.append(copy)

    spots = [t * TILE + q * STEP for t in range(STEP) for q in range(picks)]
    rest = jnp.zeros((TILE - len(spots), channels), jnp.float32)
    picked = narrow(jnp.concatenate([own[at : at + 1] for at in spots] + [rest], axis=0))
    col_blocks[own_slot + col] = picked

    @pl.when(col == half)
    def _():
        col_blocks[lax.rem(row, picks) * 2 + col] = picked

    for step in range(1, rows_axis):
        copy = col_copy(my_slot, step, {"row": lax.rem(row + step, rows_axis), "col": half})
        copy.start()
        sends.append(copy)
    copy = col_copy(own_slot + col, rows_axis, sibling)
    copy.start()
    sends.append(copy)
    extra = col_copy(my_slot, 0, sibling)

    @pl.when(col != half)
    def _():
        extra.start()

    def token_index(spot):
        inner = jnp.where(spot < width, col * width + spot, row * STEP + spot - width)
        return jnp.where(spot < width + STEP, inner, -1)

    summed = rows_axis
    n_left = summed * summed
    place = iota((n_left, 1), 0)
    a, k = place // summed, place % summed
    left_from = (a * 2 + k // picks) * TILE + k % picks * STEP
    place = iota((summed * TILE, 1), 0)
    a, j = place // TILE, place % TILE
    inside = jnp.where(
        j < width, (a * 2 + col) * TILE + j, (a * 2 + half) * TILE + STEP * (row % picks) + j - width
    )
    cross_from = jnp.where(j < width + STEP, inside, -1)
    select_rows = jnp.concatenate(
        [one_hot(left_from, devices * TILE), one_hot(cross_from, devices * TILE)], axis=0
    )
    slots = (own_slot + 2) * TILE
    place = iota((STEP * summed, 1), 0)
    t, k = place // summed, place % summed
    mine_from = (own_slot + k // picks) * TILE + t * picks + k % picks
    place = iota((summed * TILE, 1), 0)
    k, j = place // TILE, place % TILE
    inside = jnp.where(
        j < width,
        (j // STEP * 2 + k // picks) * TILE + j % STEP * picks + k % picks,
        (own_slot + k // picks) * TILE + (j - width) * picks + k % picks,
    )
    right_from = jnp.where(j < width + STEP, inside, -1)
    select_cols = jnp.concatenate([one_hot(mine_from, slots), one_hot(right_from, slots)], axis=0)

    for load in loads[1:4]:
        load.wait()
    lanes = iota((1, total), 1)
    valid = jnp.where((mask_v[...] > 0) & (lanes < count_v[0]), 1.0, 0.0)

    def pair_mask(first_index, second_index):
        grid = iota((first_index.shape[0], total), 1)
        both = jnp.where(grid == first_index, valid, 0.0) + jnp.where(
            grid == second_index, valid, 0.0
        )
        return jnp.where(jnp.sum(both, axis=-1, keepdims=True) > 1.5, 1.0, 0.0)

    place = iota(((summed + STEP) * summed, 1), 0)
    a, k = place // summed, place % summed
    left_mask = pair_mask(jnp.where(a < summed, STEP * a, row * STEP + a - summed), STEP * k)
    place = iota((summed * TILE, 1), 0)
    right_mask = pair_mask(token_index(place % TILE), STEP * (place // TILE))

    for load in loads[4:]:
        load.wait()

    for peer, where in peers:
        row_copy(peer, 0, where).wait_recv()
    for slot in range(own_slot):
        source = col * picks * 2 + slot

        @pl.when(source != me)
        def _():
            col_copy(slot, 0, sibling).wait_recv()

    col_copy(own_slot + 1 - col, 0, sibling).wait_recv()

    from_rows = dot(select_rows, row_blocks[...].reshape(devices * TILE, channels))
    from_cols = dot(select_cols, col_blocks[...].reshape(slots, channels))
    n_cross = summed * TILE
    block = jnp.concatenate([from_rows[n_left:], own], axis=0)
    normed = narrow(layer_norm(block, gain_v[0, 0][None]))
    side = jnp.concatenate([from_rows[:n_left], from_cols], axis=0)
    side = narrow(layer_norm(side, gain_v[0, 0][None]))
    n_side = n_left + STEP * summed
    gate = sigmoid(dot(normed, gate_v[0]))

    def gated(values, which, form, mask):
        value = dot(values, in_v[form, :, which * channels : (which + 1) * channels])
        opened = dot(values, in_v[form, :, (which + 2) * channels : (which + 3) * channels])
        return rounded(sigmoid(opened) * value * mask)

    left_v[0:n_side] = gated(side[:n_side], 0, 0, left_mask)
    right = gated(side[n_side:], 1, 0, right_mask)

    def finished(block, product, gate, form):
        scaled = narrow(layer_norm(rounded(product), gain_v[form, 1][None]))
        return rounded(block + dot(scaled, out_v[form]) * gate)

    def multiplied(row_of, count):
        products = []
        for a in range(count):
            acc = None
            for k in range(summed):
                at = row_of(a, k)
                term = left_v[at : at + 1] * right[k * TILE : (k + 1) * TILE]
                acc = term if acc is None else acc + term
            products.append(acc)
        return jnp.concatenate(products, axis=0)

    first = finished(block, multiplied(lambda a, k: a * summed + k, summed + STEP), gate, 0)

    normed = narrow(layer_norm(first, gain_v[1, 0][None]))
    gate = sigmoid(dot(normed[n_cross:], gate_v[1]))
    left_v[0:n_cross] = gated(normed[:n_cross], 0, 1, right_mask)
    right = gated(normed[:n_cross], 1, 1, right_mask)
    product = multiplied(lambda a, k: k * TILE + width + a, STEP)
    result = narrow(finished(first[n_cross:], product, gate, 1))
    for t in range(STEP):
        result_ref[t] = result[t * TILE : t * TILE + width]

    for copy in sends:
        copy.wait_send()

    @pl.when(col != half)
    def _():
        extra.wait_send()


def fused(pair, pad_mask, token_count, norm_gain, proj_in, proj_out, gate_out):
    rows, width, channels = pair.shape
    rows_axis = lax.axis_size("row")
    devices = 2 * rows_axis
    picks = width // STEP
    slots = 2 * picks + 2
    args = (
        pair,
        pad_mask.reshape(1, -1),
        token_count,
        norm_gain,
        proj_in,
        proj_out,
        gate_out,
    )
    return pl.pallas_call(
        functools.partial(fused_kernel, rows_axis, width),
        out_shape=pltpu.VMEM(pair.shape, pair.dtype),
        in_specs=[pl.BlockSpec(memory_space=pl.ANY)] * len(args),
        out_specs=pl.BlockSpec(memory_space=pltpu.VMEM),
        scratch_shapes=[
            (pltpu.SMEM if arg is token_count else pltpu.VMEM)(arg.shape, arg.dtype) for arg in args
        ]
        + [
            pltpu.VMEM((devices, TILE, channels), jnp.bfloat16),
            pltpu.VMEM((slots, TILE, channels), jnp.bfloat16),
            pltpu.VMEM((rows_axis * TILE, channels), jnp.float32),
            pltpu.SemaphoreType.DMA((len(args),)),
            pltpu.SemaphoreType.DMA((devices - 1,)),
            pltpu.SemaphoreType.DMA((devices,)),
            pltpu.SemaphoreType.DMA((rows_axis + 1,)),
            pltpu.SemaphoreType.DMA((slots,)),
        ],
        compiler_params=pltpu.CompilerParams(
            collective_id=0, has_side_effects=True, vmem_limit_bytes=56 * 1024 * 1024
        ),
        name="fused",
    )(*args)


def pick(mesh):
    def apply(pair, *rest):
        rows, width, _ = pair.shape
        rows_axis = mesh.shape["row"]
        small = (
            rows == STEP
            and mesh.shape["col"] == 2
            and 2 * width == STEP * rows_axis
            and width % STEP == 0
            and width + STEP <= TILE
        )
        return (fused if small else shards)(pair, *rest)

    return apply


def solution(mesh):
    in_specs = (P(("groups", "row"), "col", None), P("groups"), P("groups"), P(), P(), P(), P())
    out_specs = P(("groups", "row"), "col", None)
    return jax.shard_map(
        pick(mesh),
        mesh=mesh,
        in_specs=in_specs,
        out_specs=out_specs,
        check_vma=False,
    )
```

```python
import functools

import jax
import jax.numpy as jnp
from jax import lax
from jax.experimental import pallas as pl
from jax.experimental.pallas import tpu as pltpu
from jax.sharding import PartitionSpec as P

EPSILON = 1e-05
STEP = 3
TILE = 16
MESH = pl.DeviceIdType.MESH


def from_partner(value, axis, bit):
    mask = 2**bit
    pairs = [(source, source ^ mask) for source in range(lax.axis_size(axis))]
    return lax.ppermute(value, axis, pairs)


def layer_norm(values, gain):
    mean = jnp.mean(values, axis=-1, keepdims=True)
    centred = values - mean
    spread = jnp.mean(centred * centred, axis=-1, keepdims=True)
    return centred * lax.rsqrt(spread + EPSILON) * gain


def gated_pair(normed, weight, mask_grid):
    hidden = jnp.einsum("rnc,cd->rnd", normed, weight, preferred_element_type=jnp.float32)
    width = weight.shape[0]
    left = (
        jax.nn.sigmoid(hidden[..., 2 * width : 3 * width])
        * hidden[..., :width]
        * mask_grid[..., None]
    )
    right = (
        jax.nn.sigmoid(hidden[..., 3 * width :])
        * hidden[..., width : 2 * width]
        * mask_grid[..., None]
    )
    return (left.astype(jnp.bfloat16), right.astype(jnp.bfloat16))


def spread_out(left, right):
    moved = (
        lax.all_to_all(
            jnp.transpose(left, (2, 0, 1)), "row", split_axis=0, concat_axis=1, tiled=True
        ),
        lax.all_to_all(
            jnp.transpose(right, (2, 0, 1)), "row", split_axis=0, concat_axis=1, tiled=True
        ),
    )
    return (moved[0], moved[1])


def bring_back(product):
    moved = lax.all_to_all(product, "row", split_axis=1, concat_axis=0, tiled=True)
    return jnp.transpose(moved, (1, 2, 0))


def finish(pair, normed, product, gain_out, weight_out, weight_gate):
    gate = jax.nn.sigmoid(
        jnp.einsum("rnc,cd->rnd", normed, weight_gate, preferred_element_type=jnp.float32)
    )
    scaled = layer_norm(product.astype(jnp.float32), gain_out).astype(jnp.bfloat16)
    update = (
        jnp.einsum("rnc,cd->rnd", scaled, weight_out, preferred_element_type=jnp.float32) * gate
    )
    return (pair.astype(jnp.float32) + update).astype(jnp.bfloat16)


def outgoing(pair, row_valid, col_valid, gains, weight_in, weight_out, weight_gate):
    rows, width_cols, channels = pair.shape
    normed = layer_norm(pair.astype(jnp.float32), gains[0]).astype(jnp.bfloat16)
    picked = normed.reshape(rows, width_cols // 3, 3, channels)[:, :, 0]
    mask_grid = row_valid[:, None] * col_valid.reshape(width_cols // 3, 3)[:, 0][None, :]
    left, right = gated_pair(picked, weight_in, mask_grid)
    left, right = spread_out(left, right)
    col_index = lax.axis_index("col")
    full_left, every_right = (
        lax.all_gather(left, "col", axis=2, tiled=True),
        lax.all_gather(right, "col", axis=2, tiled=True),
    )
    full_right = lax.dynamic_slice_in_dim(every_right, col_index * width_cols, width_cols, 1)
    product = jnp.einsum("cik,cjk->cij", full_left, full_right, preferred_element_type=jnp.float32)
    product = bring_back(product.astype(jnp.bfloat16))
    return finish(pair, normed, product, gains[1], weight_out, weight_gate)


def incoming(pair, row_valid, col_valid, gains, weight_in, weight_out, weight_gate):
    rows, width_cols, channels = pair.shape
    normed = layer_norm(pair.astype(jnp.float32), gains[0]).astype(jnp.bfloat16)
    picked = normed.reshape(rows // 3, 3, width_cols, channels)[:, 0]
    mask_grid = row_valid.reshape(rows // 3, 3)[:, 0][:, None] * col_valid[None, :]
    left, right = gated_pair(picked, weight_in, mask_grid)
    left, right = spread_out(left, right)
    col_index = lax.axis_index("col")
    got = from_partner(left, "col", 0)
    full_left = jnp.where(
        col_index == 0, jnp.concatenate([left, got], axis=2), jnp.concatenate([got, left], axis=2)
    )
    product = jnp.einsum("cki,ckj->cij", full_left, right, preferred_element_type=jnp.float32)
    product = bring_back(product.astype(jnp.bfloat16))
    return finish(pair, normed, product, gains[1], weight_out, weight_gate)


def shards(pair, pad_mask, token_count, norm_gain, proj_in, proj_out, gate_out):
    rows, width_cols, channels = pair.shape
    total = pad_mask.shape[0]
    positions = jnp.arange(total, dtype=jnp.int32)
    valid = jnp.where((pad_mask > 0) & (positions < token_count[0]), 1.0, 0.0).astype(jnp.float32)
    row_valid = lax.dynamic_slice_in_dim(valid, lax.axis_index("row") * rows, rows)
    col_valid = lax.dynamic_slice_in_dim(valid, lax.axis_index("col") * width_cols, width_cols)
    first = outgoing(pair, row_valid, col_valid, norm_gain[0], proj_in[0], proj_out[0], gate_out[0])
    return incoming(first, row_valid, col_valid, norm_gain[1], proj_in[1], proj_out[1], gate_out[1])


def sigmoid(values):
    return 0.5 * jnp.tanh(0.5 * values) + 0.5


def narrow(values):
    return values.astype(jnp.bfloat16)


def rounded(values):
    return values.astype(jnp.bfloat16).astype(jnp.float32)


def dot(left, right):
    return jnp.dot(left, right, preferred_element_type=jnp.float32)


def iota(shape, axis):
    return lax.broadcasted_iota(jnp.int32, shape, axis)


def one_hot(index, width):
    return narrow(jnp.where(iota((index.shape[0], width), 1) == index, 1.0, 0.0))


def fused_kernel(
    rows_axis,
    width,
    pair_hbm,
    mask_hbm,
    count_hbm,
    gain_hbm,
    in_hbm,
    out_hbm,
    gate_hbm,
    result_ref,
    pair_v,
    mask_v,
    count_v,
    gain_v,
    in_v,
    out_v,
    gate_v,
    row_blocks,
    col_blocks,
    left_v,
    load_sem,
    send_row,
    recv_row,
    send_col,
    recv_col,
):
    channels = pair_v.shape[-1]
    total = STEP * rows_axis
    picks = width // STEP
    devices = 2 * rows_axis
    row = lax.axis_index("row")
    col = lax.axis_index("col")
    me = row * 2 + col
    half = row // picks
    own_slot = 2 * picks

    loads = [
        pltpu.make_async_copy(source, target, load_sem.at[at])
        for at, (source, target) in enumerate(
            [
                (pair_hbm, pair_v),
                (mask_hbm, mask_v),
                (count_hbm, count_v),
                (gain_hbm, gain_v),
                (in_hbm, in_v),
                (out_hbm, out_v),
                (gate_hbm, gate_v),
            ]
        )
    ]
    loads[0].start()

    col_blocks[...] = jnp.zeros_like(col_blocks)
    peers = []
    for offset in range(1, devices):
        peer = lax.rem(me + offset, devices)
        peers.append((peer, {"row": peer // 2, "col": lax.rem(peer, 2)}))
    barrier = pltpu.get_barrier_semaphore()
    for _, where in peers:
        pl.semaphore_signal(barrier, inc=1, device_id=where, device_id_type=MESH)
    for load in loads[1:]:
        load.start()

    loads[0].wait()
    pad = jnp.zeros((TILE - width, channels), jnp.float32)
    own = jnp.concatenate(
        [piece for t in range(STEP) for piece in (pair_v[t].astype(jnp.float32), pad)], axis=0
    )
    row_blocks[me] = narrow(own[:TILE])
    pl.semaphore_wait(barrier, devices - 1)

    def row_copy(block, slot, where):
        return pltpu.make_async_remote_copy(
            src_ref=row_blocks.at[me],
            dst_ref=row_blocks.at[block],
            send_sem=send_row.at[slot],
            recv_sem=recv_row.at[block],
            device_id=where,
            device_id_type=MESH,
        )

    def col_copy(block, slot, where):
        return pltpu.make_async_remote_copy(
            src_ref=col_blocks.at[own_slot + col],
            dst_ref=col_blocks.at[block],
            send_sem=send_col.at[slot],
            recv_sem=recv_col.at[block],
            device_id=where,
            device_id_type=MESH,
        )

    sends = []
    my_slot = lax.rem(row, picks) * 2 + col
    sibling = {"row": row, "col": 1 - col}

    spots = [t * TILE + q * STEP for t in range(STEP) for q in range(picks)]
    rest = jnp.zeros((TILE - len(spots), channels), jnp.float32)
    picked = narrow(jnp.concatenate([own[at : at + 1] for at in spots] + [rest], axis=0))
    col_blocks[own_slot + col] = picked

    @pl.when(col == half)
    def _():
        col_blocks[lax.rem(row, picks) * 2 + col] = picked

    for step in range(rows_axis):
        ahead = [at for at in (2 * step - 1, 2 * step) if 0 <= at < devices - 1]
        for at in ahead:
            copy = row_copy(me, at, peers[at][1])
            copy.start()
            sends.append(copy)
        if step:
            where = {"row": lax.rem(row + step, rows_axis), "col": half}
            copy = col_copy(my_slot, step, where)
            copy.start()
            sends.append(copy)
    copy = col_copy(own_slot + col, rows_axis, sibling)
    copy.start()
    sends.append(copy)
    extra = col_copy(my_slot, 0, sibling)

    @pl.when(col != half)
    def _():
        extra.start()

    def token_index(spot):
        inner = jnp.where(spot < width, col * width + spot, row * STEP + spot - width)
        return jnp.where(spot < width + STEP, inner, -1)

    summed = rows_axis
    n_left = summed * summed
    place = iota((n_left, 1), 0)
    a, k = place // summed, place % summed
    left_from = (a * 2 + k // picks) * TILE + k % picks * STEP
    place = iota((summed * TILE, 1), 0)
    a, j = place // TILE, place % TILE
    inside = jnp.where(
        j < width, (a * 2 + col) * TILE + j, (a * 2 + half) * TILE + STEP * (row % picks) + j - width
    )
    cross_from = jnp.where(j < width + STEP, inside, -1)
    select_rows = jnp.concatenate(
        [one_hot(left_from, devices * TILE), one_hot(cross_from, devices * TILE)], axis=0
    )
    slots = (own_slot + 2) * TILE
    place = iota((STEP * summed, 1), 0)
    t, k = place // summed, place % summed
    mine_from = (own_slot + k // picks) * TILE + t * picks + k % picks
    place = iota((summed * TILE, 1), 0)
    k, j = place // TILE, place % TILE
    inside = jnp.where(
        j < width,
        (j // STEP * 2 + k // picks) * TILE + j % STEP * picks + k % picks,
        (own_slot + k // picks) * TILE + (j - width) * picks + k % picks,
    )
    right_from = jnp.where(j < width + STEP, inside, -1)
    select_cols = jnp.concatenate([one_hot(mine_from, slots), one_hot(right_from, slots)], axis=0)

    for load in loads[1:4]:
        load.wait()
    lanes = iota((1, total), 1)
    valid = jnp.where((mask_v[...] > 0) & (lanes < count_v[0]), 1.0, 0.0)

    def pair_mask(first_index, second_index):
        grid = iota((first_index.shape[0], total), 1)
        both = jnp.where(grid == first_index, valid, 0.0) + jnp.where(
            grid == second_index, valid, 0.0
        )
        return jnp.where(jnp.sum(both, axis=-1, keepdims=True) > 1.5, 1.0, 0.0)

    place = iota(((summed + STEP) * summed, 1), 0)
    a, k = place // summed, place % summed
    left_mask = pair_mask(jnp.where(a < summed, STEP * a, row * STEP + a - summed), STEP * k)
    place = iota((summed * TILE, 1), 0)
    right_mask = pair_mask(token_index(place % TILE), STEP * (place // TILE))

    for load in loads[4:]:
        load.wait()

    for copy in sends:
        copy.wait_send()

    @pl.when(col != half)
    def _():
        extra.wait_send()

    gate_own = sigmoid(dot(narrow(layer_norm(own, gain_v[0, 0][None])), gate_v[0]))

    for peer, where in peers:
        row_copy(peer, 0, where).wait_recv()
    for slot in range(own_slot):
        source = col * picks * 2 + slot

        @pl.when(source != me)
        def _():
            col_copy(slot, 0, sibling).wait_recv()

    col_copy(own_slot + 1 - col, 0, sibling).wait_recv()

    from_rows = dot(select_rows, row_blocks[...].reshape(devices * TILE, channels))
    from_cols = dot(select_cols, col_blocks[...].reshape(slots, channels))
    n_cross = summed * TILE
    block = jnp.concatenate([from_rows[n_left:], own], axis=0)
    normed = narrow(layer_norm(from_rows[n_left:], gain_v[0, 0][None]))
    side = jnp.concatenate([from_rows[:n_left], from_cols], axis=0)
    side = narrow(layer_norm(side, gain_v[0, 0][None]))
    n_side = n_left + STEP * summed
    gate = jnp.concatenate([sigmoid(dot(normed, gate_v[0])), gate_own], axis=0)

    def gated(values, which, form, mask):
        value = dot(values, in_v[form, :, which * channels : (which + 1) * channels])
        opened = dot(values, in_v[form, :, (which + 2) * channels : (which + 3) * channels])
        return rounded(sigmoid(opened) * value * mask)

    left_v[0:n_side] = gated(side[:n_side], 0, 0, left_mask)
    right = gated(side[n_side:], 1, 0, right_mask)

    def finished(block, product, gate, form):
        scaled = narrow(layer_norm(rounded(product), gain_v[form, 1][None]))
        return rounded(block + dot(scaled, out_v[form]) * gate)

    def multiplied(row_of, count):
        products = []
        for a in range(count):
            acc = None
            for k in range(summed):
                at = row_of(a, k)
                term = left_v[at : at + 1] * right[k * TILE : (k + 1) * TILE]
                acc = term if acc is None else acc + term
            products.append(acc)
        return jnp.concatenate(products, axis=0)

    first = finished(block, multiplied(lambda a, k: a * summed + k, summed + STEP), gate, 0)

    normed = narrow(layer_norm(first, gain_v[1, 0][None]))
    gate = sigmoid(dot(normed[n_cross:], gate_v[1]))
    left_v[0:n_cross] = gated(normed[:n_cross], 0, 1, right_mask)
    right = gated(normed[:n_cross], 1, 1, right_mask)
    product = multiplied(lambda a, k: k * TILE + width + a, STEP)
    result = narrow(finished(first[n_cross:], product, gate, 1))
    for t in range(STEP):
        result_ref[t] = result[t * TILE : t * TILE + width]


def fused(pair, pad_mask, token_count, norm_gain, proj_in, proj_out, gate_out):
    rows, width, channels = pair.shape
    rows_axis = lax.axis_size("row")
    devices = 2 * rows_axis
    picks = width // STEP
    slots = 2 * picks + 2
    args = (
        pair,
        pad_mask.reshape(1, -1),
        token_count,
        norm_gain,
        proj_in,
        proj_out,
        gate_out,
    )
    return pl.pallas_call(
        functools.partial(fused_kernel, rows_axis, width),
        out_shape=pltpu.VMEM(pair.shape, pair.dtype),
        in_specs=[pl.BlockSpec(memory_space=pl.ANY)] * len(args),
        out_specs=pl.BlockSpec(memory_space=pltpu.VMEM),
        scratch_shapes=[
            (pltpu.SMEM if arg is token_count else pltpu.VMEM)(arg.shape, arg.dtype) for arg in args
        ]
        + [
            pltpu.VMEM((devices, TILE, channels), jnp.bfloat16),
            pltpu.VMEM((slots, TILE, channels), jnp.bfloat16),
            pltpu.VMEM((rows_axis * TILE, channels), jnp.float32),
            pltpu.SemaphoreType.DMA((len(args),)),
            pltpu.SemaphoreType.DMA((devices - 1,)),
            pltpu.SemaphoreType.DMA((devices,)),
            pltpu.SemaphoreType.DMA((rows_axis + 1,)),
            pltpu.SemaphoreType.DMA((slots,)),
        ],
        compiler_params=pltpu.CompilerParams(
            collective_id=0, has_side_effects=True, vmem_limit_bytes=56 * 1024 * 1024
        ),
        name="fused",
    )(*args)


def pick(mesh):
    def apply(pair, *rest):
        rows, width, _ = pair.shape
        rows_axis = mesh.shape["row"]
        small = (
            rows == STEP
            and mesh.shape["col"] == 2
            and 2 * width == STEP * rows_axis
            and width % STEP == 0
            and width + STEP <= TILE
        )
        return (fused if small else shards)(pair, *rest)

    return apply


def solution(mesh):
    in_specs = (P(("groups", "row"), "col", None), P("groups"), P("groups"), P(), P(), P(), P())
    out_specs = P(("groups", "row"), "col", None)
    return jax.shard_map(
        pick(mesh),
        mesh=mesh,
        in_specs=in_specs,
        out_specs=out_specs,
        check_vma=False,
    )
```

```python
import functools

import jax
import jax.numpy as jnp
from jax import lax
from jax.experimental import pallas as pl
from jax.experimental.pallas import tpu as pltpu
from jax.sharding import PartitionSpec as P

EPSILON = 1e-05
STEP = 3
TILE = 16
MESH = pl.DeviceIdType.MESH


def from_partner(value, axis, bit):
    mask = 2**bit
    pairs = [(source, source ^ mask) for source in range(lax.axis_size(axis))]
    return lax.ppermute(value, axis, pairs)


def layer_norm(values, gain):
    mean = jnp.mean(values, axis=-1, keepdims=True)
    centred = values - mean
    spread = jnp.mean(centred * centred, axis=-1, keepdims=True)
    return centred * lax.rsqrt(spread + EPSILON) * gain


def gated_pair(normed, weight, mask_grid):
    hidden = jnp.einsum("rnc,cd->rnd", normed, weight, preferred_element_type=jnp.float32)
    width = weight.shape[0]
    left = (
        jax.nn.sigmoid(hidden[..., 2 * width : 3 * width])
        * hidden[..., :width]
        * mask_grid[..., None]
    )
    right = (
        jax.nn.sigmoid(hidden[..., 3 * width :])
        * hidden[..., width : 2 * width]
        * mask_grid[..., None]
    )
    return (left.astype(jnp.bfloat16), right.astype(jnp.bfloat16))


def spread_out(left, right):
    moved = (
        lax.all_to_all(
            jnp.transpose(left, (2, 0, 1)), "row", split_axis=0, concat_axis=1, tiled=True
        ),
        lax.all_to_all(
            jnp.transpose(right, (2, 0, 1)), "row", split_axis=0, concat_axis=1, tiled=True
        ),
    )
    return (moved[0], moved[1])


def bring_back(product):
    moved = lax.all_to_all(product, "row", split_axis=1, concat_axis=0, tiled=True)
    return jnp.transpose(moved, (1, 2, 0))


def finish(pair, normed, product, gain_out, weight_out, weight_gate):
    gate = jax.nn.sigmoid(
        jnp.einsum("rnc,cd->rnd", normed, weight_gate, preferred_element_type=jnp.float32)
    )
    scaled = layer_norm(product.astype(jnp.float32), gain_out).astype(jnp.bfloat16)
    update = (
        jnp.einsum("rnc,cd->rnd", scaled, weight_out, preferred_element_type=jnp.float32) * gate
    )
    return (pair.astype(jnp.float32) + update).astype(jnp.bfloat16)


def outgoing(pair, row_valid, col_valid, gains, weight_in, weight_out, weight_gate):
    rows, width_cols, channels = pair.shape
    normed = layer_norm(pair.astype(jnp.float32), gains[0]).astype(jnp.bfloat16)
    picked = normed.reshape(rows, width_cols // 3, 3, channels)[:, :, 0]
    mask_grid = row_valid[:, None] * col_valid.reshape(width_cols // 3, 3)[:, 0][None, :]
    left, right = gated_pair(picked, weight_in, mask_grid)
    left, right = spread_out(left, right)
    col_index = lax.axis_index("col")
    full_left, every_right = (
        lax.all_gather(left, "col", axis=2, tiled=True),
        lax.all_gather(right, "col", axis=2, tiled=True),
    )
    full_right = lax.dynamic_slice_in_dim(every_right, col_index * width_cols, width_cols, 1)
    product = jnp.einsum("cik,cjk->cij", full_left, full_right, preferred_element_type=jnp.float32)
    product = bring_back(product.astype(jnp.bfloat16))
    return finish(pair, normed, product, gains[1], weight_out, weight_gate)


def incoming(pair, row_valid, col_valid, gains, weight_in, weight_out, weight_gate):
    rows, width_cols, channels = pair.shape
    normed = layer_norm(pair.astype(jnp.float32), gains[0]).astype(jnp.bfloat16)
    picked = normed.reshape(rows // 3, 3, width_cols, channels)[:, 0]
    mask_grid = row_valid.reshape(rows // 3, 3)[:, 0][:, None] * col_valid[None, :]
    left, right = gated_pair(picked, weight_in, mask_grid)
    left, right = spread_out(left, right)
    col_index = lax.axis_index("col")
    got = from_partner(left, "col", 0)
    full_left = jnp.where(
        col_index == 0, jnp.concatenate([left, got], axis=2), jnp.concatenate([got, left], axis=2)
    )
    product = jnp.einsum("cki,ckj->cij", full_left, right, preferred_element_type=jnp.float32)
    product = bring_back(product.astype(jnp.bfloat16))
    return finish(pair, normed, product, gains[1], weight_out, weight_gate)


def shards(pair, pad_mask, token_count, norm_gain, proj_in, proj_out, gate_out):
    rows, width_cols, channels = pair.shape
    total = pad_mask.shape[0]
    positions = jnp.arange(total, dtype=jnp.int32)
    valid = jnp.where((pad_mask > 0) & (positions < token_count[0]), 1.0, 0.0).astype(jnp.float32)
    row_valid = lax.dynamic_slice_in_dim(valid, lax.axis_index("row") * rows, rows)
    col_valid = lax.dynamic_slice_in_dim(valid, lax.axis_index("col") * width_cols, width_cols)
    first = outgoing(pair, row_valid, col_valid, norm_gain[0], proj_in[0], proj_out[0], gate_out[0])
    return incoming(first, row_valid, col_valid, norm_gain[1], proj_in[1], proj_out[1], gate_out[1])


def sigmoid(values):
    return 0.5 * jnp.tanh(0.5 * values) + 0.5


def narrow(values):
    return values.astype(jnp.bfloat16)


def rounded(values):
    return values.astype(jnp.bfloat16).astype(jnp.float32)


def dot(left, right):
    return jnp.dot(left, right, preferred_element_type=jnp.float32)


def iota(shape, axis):
    return lax.broadcasted_iota(jnp.int32, shape, axis)


def one_hot(index, width):
    return narrow(jnp.where(iota((index.shape[0], width), 1) == index, 1.0, 0.0))


def fused_kernel(
    rows_axis,
    width,
    pair_hbm,
    mask_hbm,
    count_hbm,
    gain_hbm,
    in_hbm,
    out_hbm,
    gate_hbm,
    result_ref,
    pair_v,
    mask_v,
    count_v,
    gain_v,
    in_v,
    out_v,
    gate_v,
    row_blocks,
    col_blocks,
    left_v,
    load_sem,
    send_row,
    recv_row,
    send_col,
    recv_col,
):
    channels = pair_v.shape[-1]
    total = STEP * rows_axis
    picks = width // STEP
    devices = 2 * rows_axis
    row = lax.axis_index("row")
    col = lax.axis_index("col")
    me = row * 2 + col
    half = row // picks
    own_slot = 2 * picks

    loads = [
        pltpu.make_async_copy(source, target, load_sem.at[at])
        for at, (source, target) in enumerate(
            [
                (pair_hbm, pair_v),
                (mask_hbm, mask_v),
                (count_hbm, count_v),
                (gain_hbm, gain_v),
                (in_hbm, in_v),
                (out_hbm, out_v),
                (gate_hbm, gate_v),
            ]
        )
    ]
    loads[0].start()

    col_blocks[...] = jnp.zeros_like(col_blocks)
    peers = []
    for offset in range(1, devices):
        peer = lax.rem(me + offset, devices)
        peers.append((peer, {"row": peer // 2, "col": lax.rem(peer, 2)}))
    barrier = pltpu.get_barrier_semaphore()
    for _, where in peers:
        pl.semaphore_signal(barrier, inc=1, device_id=where, device_id_type=MESH)
    for load in loads[1:]:
        load.start()

    loads[0].wait()
    pad = jnp.zeros((TILE - width, channels), jnp.float32)
    own = jnp.concatenate(
        [piece for t in range(STEP) for piece in (pair_v[t].astype(jnp.float32), pad)], axis=0
    )
    row_blocks[me] = narrow(own[:TILE])
    pl.semaphore_wait(barrier, devices - 1)

    def row_copy(block, slot, where):
        return pltpu.make_async_remote_copy(
            src_ref=row_blocks.at[me],
            dst_ref=row_blocks.at[block],
            send_sem=send_row.at[slot],
            recv_sem=recv_row.at[block],
            device_id=where,
            device_id_type=MESH,
        )

    def col_copy(block, slot, where):
        return pltpu.make_async_remote_copy(
            src_ref=col_blocks.at[own_slot + col],
            dst_ref=col_blocks.at[block],
            send_sem=send_col.at[slot],
            recv_sem=recv_col.at[block],
            device_id=where,
            device_id_type=MESH,
        )

    sends = []
    my_slot = lax.rem(row, picks) * 2 + col
    sibling = {"row": row, "col": 1 - col}

    spots = [t * TILE + q * STEP for t in range(STEP) for q in range(picks)]
    rest = jnp.zeros((TILE - len(spots), channels), jnp.float32)
    picked = narrow(jnp.concatenate([own[at : at + 1] for at in spots] + [rest], axis=0))
    col_blocks[own_slot + col] = picked

    @pl.when(col == half)
    def _():
        col_blocks[lax.rem(row, picks) * 2 + col] = picked

    for step in range(rows_axis):
        ahead = [at for at in (2 * step - 1, 2 * step) if 0 <= at < devices - 1]
        for at in ahead:
            copy = row_copy(me, at, peers[at][1])
            copy.start()
            sends.append(copy)
        if step:
            where = {"row": lax.rem(row + step, rows_axis), "col": half}
            copy = col_copy(my_slot, step, where)
            copy.start()
            sends.append(copy)
    copy = col_copy(own_slot + col, rows_axis, sibling)
    copy.start()
    sends.append(copy)
    extra = col_copy(my_slot, 0, sibling)

    @pl.when(col != half)
    def _():
        extra.start()

    def token_index(spot):
        inner = jnp.where(spot < width, col * width + spot, row * STEP + spot - width)
        return jnp.where(spot < width + STEP, inner, -1)

    summed = rows_axis
    n_left = summed * summed
    place = iota((n_left, 1), 0)
    a, k = place // summed, place % summed
    left_from = (a * 2 + k // picks) * TILE + k % picks * STEP
    place = iota((summed * TILE, 1), 0)
    a, j = place // TILE, place % TILE
    inside = jnp.where(
        j < width, (a * 2 + col) * TILE + j, (a * 2 + half) * TILE + STEP * (row % picks) + j - width
    )
    cross_from = jnp.where(j < width + STEP, inside, -1)
    select_rows = jnp.concatenate(
        [one_hot(left_from, devices * TILE), one_hot(cross_from, devices * TILE)], axis=0
    )
    slots = (own_slot + 2) * TILE
    place = iota((STEP * summed, 1), 0)
    t, k = place // summed, place % summed
    mine_from = (own_slot + k // picks) * TILE + t * picks + k % picks
    place = iota((summed * TILE, 1), 0)
    k, j = place // TILE, place % TILE
    inside = jnp.where(
        j < width,
        (j // STEP * 2 + k // picks) * TILE + j % STEP * picks + k % picks,
        (own_slot + k // picks) * TILE + (j - width) * picks + k % picks,
    )
    right_from = jnp.where(j < width + STEP, inside, -1)
    select_cols = jnp.concatenate([one_hot(mine_from, slots), one_hot(right_from, slots)], axis=0)

    for load in loads[1:4]:
        load.wait()
    lanes = iota((1, total), 1)
    valid = jnp.where((mask_v[...] > 0) & (lanes < count_v[0]), 1.0, 0.0)

    def pair_mask(first_index, second_index):
        grid = iota((first_index.shape[0], total), 1)
        both = jnp.where(grid == first_index, valid, 0.0) + jnp.where(
            grid == second_index, valid, 0.0
        )
        return jnp.where(jnp.sum(both, axis=-1, keepdims=True) > 1.5, 1.0, 0.0)

    place = iota(((summed + STEP) * summed, 1), 0)
    a, k = place // summed, place % summed
    left_mask = pair_mask(jnp.where(a < summed, STEP * a, row * STEP + a - summed), STEP * k)
    place = iota((summed * TILE, 1), 0)
    right_mask = pair_mask(token_index(place % TILE), STEP * (place // TILE))

    for load in loads[4:]:
        load.wait()

    for copy in sends:
        copy.wait_send()

    @pl.when(col != half)
    def _():
        extra.wait_send()

    gate_own = sigmoid(dot(narrow(layer_norm(own, gain_v[0, 0][None])), gate_v[0]))

    for peer, where in peers:
        row_copy(peer, 0, where).wait_recv()
    for slot in range(own_slot):
        source = col * picks * 2 + slot

        @pl.when(source != me)
        def _():
            col_copy(slot, 0, sibling).wait_recv()

    col_copy(own_slot + 1 - col, 0, sibling).wait_recv()

    from_rows = dot(select_rows, row_blocks[...].reshape(devices * TILE, channels))
    from_cols = dot(select_cols, col_blocks[...].reshape(slots, channels))
    n_cross = summed * TILE
    block = jnp.concatenate([from_rows[n_left:], own], axis=0)
    normed = narrow(layer_norm(from_rows[n_left:], gain_v[0, 0][None]))
    side = jnp.concatenate([from_rows[:n_left], from_cols], axis=0)
    side = narrow(layer_norm(side, gain_v[0, 0][None]))
    n_side = n_left + STEP * summed
    gate = jnp.concatenate([sigmoid(dot(normed, gate_v[0])), gate_own], axis=0)

    def gated(values, which, form, mask):
        spans = [slice(at * channels, (at + 1) * channels) for at in (which, which + 2)]
        hidden = dot(values, jnp.concatenate([in_v[form, :, span] for span in spans], axis=1))
        value, opened = hidden[:, :channels], hidden[:, channels:]
        return rounded(sigmoid(opened) * value * mask)

    left_v[0:n_side] = gated(side[:n_side], 0, 0, left_mask)
    right = gated(side[n_side:], 1, 0, right_mask)

    def finished(block, product, gate, form):
        scaled = narrow(layer_norm(rounded(product), gain_v[form, 1][None]))
        return rounded(block + dot(scaled, out_v[form]) * gate)

    def multiplied(row_of, count):
        products = []
        for a in range(count):
            acc = None
            for k in range(summed):
                at = row_of(a, k)
                term = left_v[at : at + 1] * right[k * TILE : (k + 1) * TILE]
                acc = term if acc is None else acc + term
            products.append(acc)
        return jnp.concatenate(products, axis=0)

    first = finished(block, multiplied(lambda a, k: a * summed + k, summed + STEP), gate, 0)

    normed = narrow(layer_norm(first, gain_v[1, 0][None]))
    gate = sigmoid(dot(normed[n_cross:], gate_v[1]))
    left_v[0:n_cross] = gated(normed[:n_cross], 0, 1, right_mask)
    right = gated(normed[:n_cross], 1, 1, right_mask)
    product = multiplied(lambda a, k: k * TILE + width + a, STEP)
    result = narrow(finished(first[n_cross:], product, gate, 1))
    for t in range(STEP):
        result_ref[t] = result[t * TILE : t * TILE + width]


def fused(pair, pad_mask, token_count, norm_gain, proj_in, proj_out, gate_out):
    rows, width, channels = pair.shape
    rows_axis = lax.axis_size("row")
    devices = 2 * rows_axis
    picks = width // STEP
    slots = 2 * picks + 2
    args = (
        pair,
        pad_mask.reshape(1, -1),
        token_count,
        norm_gain,
        proj_in,
        proj_out,
        gate_out,
    )
    return pl.pallas_call(
        functools.partial(fused_kernel, rows_axis, width),
        out_shape=pltpu.VMEM(pair.shape, pair.dtype),
        in_specs=[pl.BlockSpec(memory_space=pl.ANY)] * len(args),
        out_specs=pl.BlockSpec(memory_space=pltpu.VMEM),
        scratch_shapes=[
            (pltpu.SMEM if arg is token_count else pltpu.VMEM)(arg.shape, arg.dtype) for arg in args
        ]
        + [
            pltpu.VMEM((devices, TILE, channels), jnp.bfloat16),
            pltpu.VMEM((slots, TILE, channels), jnp.bfloat16),
            pltpu.VMEM((rows_axis * TILE, channels), jnp.float32),
            pltpu.SemaphoreType.DMA((len(args),)),
            pltpu.SemaphoreType.DMA((devices - 1,)),
            pltpu.SemaphoreType.DMA((devices,)),
            pltpu.SemaphoreType.DMA((rows_axis + 1,)),
            pltpu.SemaphoreType.DMA((slots,)),
        ],
        compiler_params=pltpu.CompilerParams(
            collective_id=0, has_side_effects=True, vmem_limit_bytes=56 * 1024 * 1024
        ),
        name="fused",
    )(*args)


def pick(mesh):
    def apply(pair, *rest):
        rows, width, _ = pair.shape
        rows_axis = mesh.shape["row"]
        small = (
            rows == STEP
            and mesh.shape["col"] == 2
            and 2 * width == STEP * rows_axis
            and width % STEP == 0
            and width + STEP <= TILE
        )
        return (fused if small else shards)(pair, *rest)

    return apply


def solution(mesh):
    in_specs = (P(("groups", "row"), "col", None), P("groups"), P("groups"), P(), P(), P(), P())
    out_specs = P(("groups", "row"), "col", None)
    return jax.shard_map(
        pick(mesh),
        mesh=mesh,
        in_specs=in_specs,
        out_specs=out_specs,
        check_vma=False,
    )
```
